128 devices in a mesh: seq: 8 (over y, core), mp: 16 (over z, x).
Axes of the slice: x: 4, y: 4, z: 4, core: 2. Of those that a mesh axis runs over, the one named last changes fastest.
Arguments:
- cache: bfloat16 [4096, 64, 576], P('seq', 'mp'), may hold values from -6 to 6
- span_latents: bfloat16 [2048, 576], P('seq'), may hold values from -6 to 6
- queries: bfloat16 [2048, 73728], P('seq', 'mp'), may hold values from -12 to 12
- selected: int32 [16, 32], replicated, may hold values from 0 to 4095, as said below
- w_uv: bfloat16 [128, 512, 128], P('mp'), may hold values from -2 to 2
- w_out: bfloat16 [16384, 7168], P('mp'), may hold values from -0.4375 to 0.4375
Outputs:
- attended: bfloat16 [2048, 7168], P(('seq', 'mp'))
The draws below stay inside these ranges and needn't reach their ends.
Inputs may be any that keep to these rules, and one draw needn't show every extreme that they name: `selected`: each row names 32 different blocks. Blocks s * 512 to (s + 1) * 512 - 1 form owner s. For the rows of the groups of one seq index's tokens, one owner holds exactly 16 of every such row's blocks, so that it receives exactly 32 selections from them, and no other owner receives more than 32.
All inputs are finite; a program needn't handle non-finite values.
Results may differ from the reference program's by a relative error of at most 0.014.
Values may be sent and summed in bfloat16 or wider, within the bound.
No kernel may reach another device: no remote copies, remote signals or barrier semaphores. Data moves between devices by JAX's collectives and lax.ppermute only.
A program may use at most 128 MiB of HBM per device.

```python
import jax
import jax.numpy as jnp
from jax import lax

D = 7168
HEADS = 128
KV_RANK = 512
VDIM = 128
QK_HEAD = 192
BLOCK = 64
SEL = 32
QG = 128
TOK_DEV = 256
BLK_SEQ = 512
TOKENS = 2048
GROUPS = 16
NBLK = 4096
LAT = 576


def draw_queries(key, part):
    key = jax.random.fold_in(key, 5)
    base_key = jax.random.fold_in(key, 0)
    values = jax.random.truncated_normal(base_key, -6.0, 6.0, (TOKENS, HEADS, LAT), jnp.float32)
    return values.reshape(TOKENS, HEADS * LAT).astype(jnp.bfloat16)


def draw_span_latents(key, part):
    key = jax.random.fold_in(key, 7)
    base_key = jax.random.fold_in(key, 0)
    values = jax.random.truncated_normal(base_key, -6.0, 6.0, (TOKENS, LAT), jnp.float32)
    return values.astype(jnp.bfloat16)


def draw_selected(key, part):
    key = jax.random.fold_in(key, 11)
    hot_key, group_key = jax.random.split(key)
    owners = NBLK // BLK_SEQ
    groups_dev = TOK_DEV // QG
    hot_owner = jax.random.randint(hot_key, (owners,), 0, owners)
    block_owner = jnp.arange(NBLK, dtype=jnp.int32) // BLK_SEQ
    half = SEL // 2

    def one_group(group_seed, group):
        rank_key, order_key = jax.random.split(group_seed)
        ranks = jax.random.permutation(rank_key, NBLK).astype(jnp.int32)
        mine = block_owner == hot_owner[group // groups_dev]
        hot_vals, hot_pick = lax.top_k(jnp.where(mine, ranks, -1), half)
        cold_vals, cold_pick = lax.top_k(jnp.where(mine, -1, ranks), SEL - half)
        picks = jnp.concatenate([hot_pick, cold_pick]).astype(jnp.int32)
        order = jax.random.permutation(order_key, SEL)
        return picks[order].astype(jnp.int32)
    seeds = jax.random.split(group_key, GROUPS)
    return jax.vmap(one_group)(seeds, jnp.arange(GROUPS, dtype=jnp.int32))


def level_of(stream_key, dims, shards, smallest, top_value):
    def one(dim, blocks):
        draws = jax.random.uniform(jax.random.fold_in(jax.random.fold_in(stream_key, 6), dim), (blocks,), jnp.float32, smallest / len(shards), top_value / len(shards))
        return jnp.repeat(jnp.exp(draws), dims[dim] // blocks).reshape((-1,) + (1,) * (len(dims) - dim - 1))

    gain = one(*shards[0])
    for cut in shards[1:]:
        gain = gain * one(*cut)
    return gain


def gaussian(rng, dims, spread, limit, pieces=(), kind=jnp.bfloat16):
    entries = jax.random.normal(rng, dims, jnp.float32) * spread
    if len(pieces) > 0:
        entries = level_of(rng, dims, pieces, -0.22, 0.18) * entries
    return jnp.clip(entries, min=-limit, max=limit).astype(kind)


def setup_inputs(seed: int = 0) -> dict:
    streams_of = jax.random.split(jax.random.key(seed), 7)
    return {
        "cache": gaussian(streams_of[0], (NBLK, BLOCK, LAT), 1.0, 6.0, ((0, 8), (1, 16))),
        "span_latents": draw_span_latents(jax.random.fold_in(streams_of[6], 71), 0),
        "queries": draw_queries(jax.random.fold_in(streams_of[6], 71), 0),
        "selected": draw_selected(jax.random.fold_in(streams_of[6], 71), 0),
        "w_uv": gaussian(streams_of[4], (HEADS, KV_RANK, VDIM), 0.13, 2.0, ((0, 16),)),
        "w_out": gaussian(streams_of[5], (HEADS * VDIM, D), 0.03, 0.4375, ((0, 16),)),
    }


def reference(cache, span_latents, queries, selected, w_uv, w_out):
    scale = float(QK_HEAD) ** -0.5
    prior_count = SEL * BLOCK

    def one_group(group):
        picks = selected[group]
        prior = jnp.take(cache, picks, axis=0).reshape(prior_count, LAT)
        start = (group * QG).astype(jnp.int32)
        local = lax.dynamic_slice_in_dim(span_latents, start, QG, 0)
        keys = jnp.concatenate([prior, local], axis=0)
        qrows = lax.dynamic_slice_in_dim(queries, start, QG, 0).reshape(QG * HEADS, LAT)
        scores = jnp.dot(qrows, keys.T, preferred_element_type=jnp.float32) * scale
        row_token = lax.broadcasted_iota(jnp.int32, (QG * HEADS, prior_count + QG), 0) // HEADS
        key_slot = lax.broadcasted_iota(jnp.int32, (QG * HEADS, prior_count + QG), 1)
        allowed = (key_slot < prior_count) | (key_slot - prior_count <= row_token)
        scores = jnp.where(allowed, scores, -jnp.inf)
        top = jnp.max(scores, axis=1, keepdims=True)
        expo = jnp.exp(scores - top)
        probs = (expo / jnp.sum(expo, axis=1, keepdims=True)).astype(jnp.bfloat16)
        latent_out = jnp.dot(probs, keys[:, :KV_RANK], preferred_element_type=jnp.float32).astype(jnp.bfloat16)
        latent_out = latent_out.reshape(QG, HEADS, KV_RANK)
        head_out = jnp.einsum("thr,hrv->thv", latent_out.astype(jnp.float32), w_uv.astype(jnp.float32))
        return head_out.astype(jnp.bfloat16).reshape(QG, HEADS * VDIM)

    heads = lax.map(one_group, jnp.arange(GROUPS, dtype=jnp.int32)).reshape(TOKENS, HEADS * VDIM)
    return jnp.dot(heads, w_out, preferred_element_type=jnp.float32).astype(jnp.bfloat16)
```

```python
import jax
import jax.numpy as jnp
from jax import lax
from jax.sharding import PartitionSpec as P

KV_RANK = 512
VDIM = 128
QK_HEAD = 192
BLOCK = 64
SEL = 32
QG = 128
RING = 4
SCALE = float(QK_HEAD) ** (-0.5)


def index_of(y, core, z, x):
    return ((y * 2 + core) * RING + z) * RING + x


def pairs(move):
    out = []
    for y in range(RING):
        for core in range(2):
            for z in range(RING):
                for x in range(RING):
                    out.append((index_of(y, core, z, x), index_of(*move(y, core, z, x))))
    return out


def send(value, move):
    return lax.ppermute(value, ("seq", "mp"), pairs(move))


def along_core(value):
    return send(value, lambda y, core, z, x: (y, 1 - core, z, x))


def along_y(value, step):
    return send(value, lambda y, core, z, x: ((y + step) % RING, core, z, x))


def along_plane(value, first, step):
    def move(y, core, z, x):
        if (core == 0) == first:
            return y, core, z, (x + step) % RING
        return y, core, (z + step) % RING, x

    return send(value, move)


def body(cache, span_latents, queries, selected, w_uv, w_out):
    seq_index = lax.axis_index("seq")
    mp_index = lax.axis_index("mp")
    y_index, core = seq_index // 2, seq_index % 2
    z_index, x_index = mp_index // RING, mp_index % RING
    blocks_here, block_rows, latent_width = cache.shape
    token_count = queries.shape[0]
    heads_here = w_uv.shape[0]
    groups_here = token_count // QG
    slots = groups_here * SEL
    prior_count = SEL * BLOCK

    requests = selected.reshape(RING, 2, slots) - seq_index * blocks_here
    requests = jnp.roll(requests, -y_index, axis=0)
    requests = jnp.where(core == 0, requests, requests[:, ::-1])
    picks = requests.transpose(1, 0, 2).reshape(-1)
    onehot = (picks[:, None] == lax.broadcasted_iota(jnp.int32, (1, blocks_here), 1)).astype(
        cache.dtype
    )
    flat = cache.reshape(blocks_here, block_rows * latent_width)
    rows = jnp.dot(onehot, flat, preferred_element_type=jnp.float32).astype(cache.dtype)
    rows = rows.reshape(2, RING, slots, block_rows * latent_width)
    both = rows[0] + along_core(rows[1])
    shard = both[0] + along_y(both[1], 1) + along_y(both[2], 2) + along_y(both[3], 3)

    line = jnp.stack(
        [shard, along_plane(shard, True, 1), along_plane(shard, True, 3), along_plane(shard, True, 2)]
    )
    plane = jnp.stack(
        [line, along_plane(line, False, 1), along_plane(line, False, 3), along_plane(line, False, 2)]
    )
    plane = plane.reshape(RING * RING, groups_here, SEL, block_rows, latent_width)

    row_token = (
        lax.broadcasted_iota(jnp.int32, (QG * heads_here, prior_count + QG), 0) // heads_here
    )
    key_slot = lax.broadcasted_iota(jnp.int32, (QG * heads_here, prior_count + QG), 1)
    allowed = (key_slot < prior_count) | (key_slot - prior_count <= row_token)
    outputs = []
    for group in range(groups_here):
        prior = plane[:, group].reshape(prior_count, latent_width)
        local = span_latents[group * QG : (group + 1) * QG]
        keys = jnp.concatenate([prior, local], axis=0)
        qrows = queries[group * QG : (group + 1) * QG].reshape(QG * heads_here, latent_width)
        scores = jnp.einsum("rc,kc->rk", qrows, keys, preferred_element_type=jnp.float32) * SCALE
        scores = jnp.where(allowed, scores, -jnp.inf)
        top = jnp.max(scores, axis=1, keepdims=True)
        expo = jnp.exp(scores - top)
        probs = (expo / jnp.sum(expo, axis=1, keepdims=True)).astype(jnp.bfloat16)
        latent_out = jnp.dot(probs, keys[:, :KV_RANK], preferred_element_type=jnp.float32).astype(
            jnp.bfloat16
        )
        latent_out = latent_out.reshape(QG, heads_here, KV_RANK)
        head_out = jnp.einsum("thr,hrv->thv", latent_out, w_uv, preferred_element_type=jnp.float32)
        outputs.append(head_out.astype(jnp.bfloat16).reshape(QG, heads_here * VDIM))
    heads_all = jnp.concatenate(outputs, axis=0)

    own_rows = token_count // (RING * RING)
    first_index = jnp.where(core == 0, x_index, z_index)
    second_index = jnp.where(core == 0, z_index, x_index)
    near = heads_all.reshape(RING, RING, own_rows, heads_here * VDIM)
    near = jnp.where(core == 0, near.transpose(1, 0, 2, 3), near)
    near = jnp.roll(near, (-first_index, -second_index), axis=(0, 1))
    partial = jnp.dot(
        near.reshape(token_count, heads_here * VDIM), w_out, preferred_element_type=jnp.float32
    ).astype(jnp.bfloat16)

    def scatter(value, first):
        parts = value.reshape(RING, value.shape[0] // RING, value.shape[1])
        total = parts[0].astype(jnp.float32)
        for step in (1, 3, 2):
            total = total + along_plane(parts[step], first, step).astype(jnp.float32)
        return total.astype(jnp.bfloat16)

    return scatter(scatter(partial, True), False)


def solution(mesh):
    return jax.shard_map(
        body,
        mesh=mesh,
        in_specs=(
            P("seq", "mp", None),
            P("seq", None),
            P("seq", "mp"),
            P(),
            P("mp", None, None),
            P("mp", None),
        ),
        out_specs=P(("seq", "mp"), None),
        check_vma=False,
    )
```

```python
import functools
import math

import jax
import jax.numpy as jnp
from jax import lax
from jax.experimental import pallas as pl
from jax.experimental.pallas import tpu as pltpu
from jax.sharding import PartitionSpec as P

KV_RANK = 512
ROPE = 64
VDIM = 128
QK_HEAD = 192
BLOCK = 64
SEL = 32
QG = 128
RING = 4
ROWS = 4
KEY_WIDTH = KV_RANK + 2 * ROPE
EXP2_SCALE = float(QK_HEAD) ** (-0.5) * math.log2(math.e)
HEADS_STEP = 4
OUT_TILE = 512


def index_of(y, core, z, x):
    return ((y * 2 + core) * RING + z) * RING + x


def pairs(move):
    out = []
    for y in range(RING):
        for core in range(2):
            for z in range(RING):
                for x in range(RING):
                    out.append((index_of(y, core, z, x), index_of(*move(y, core, z, x))))
    return out


def send(value, move):
    return lax.ppermute(value, ("seq", "mp"), pairs(move))


def along_core(value):
    return send(value, lambda y, core, z, x: (y, 1 - core, z, x))


def along_y(value, step):
    return send(value, lambda y, core, z, x: ((y + step) % RING, core, z, x))


def along_plane(value, first, step):
    def move(y, core, z, x):
        if (core == 0) == first:
            return y, core, z, (x + step) % RING
        return y, core, (z + step) % RING, x

    return send(value, move)


def attend_kernel(q_even, q_odd, own, near, back, far, local, w_uv, out, keys, own_keys):
    @pl.when(pl.program_id(0) == 0)
    def _():
        for side, piece in enumerate((own, near, back, far)):
            for shard in range(RING):
                at = pl.ds((side * RING + shard) * SEL, SEL)
                for row in range(ROWS):
                    rope = ROWS * KV_RANK + (row // 2) * 2 * ROPE
                    keys[row, at, :KV_RANK] = piece[shard, :, row * KV_RANK : (row + 1) * KV_RANK]
                    keys[row, at, KV_RANK:] = piece[shard, :, rope : rope + 2 * ROPE]
        own_keys[...] = local[...]

    rows = q_even.shape[0] * QG
    even = q_even[...].reshape(rows, KEY_WIDTH)
    odd = q_odd[...].reshape(rows, KEY_WIDTH)
    contract = (((1,), (1,)), ((), ()))
    scores = [
        lax.dot_general(
            even if row % 2 == 0 else odd, keys[row], contract, preferred_element_type=jnp.float32
        )
        for row in range(ROWS)
    ]
    inside = lax.dot_general(even, own_keys[...], contract, preferred_element_type=jnp.float32)
    token = lax.broadcasted_iota(jnp.int32, (rows, QG), 0) % QG
    slot = lax.broadcasted_iota(jnp.int32, (rows, QG), 1)
    scores.append(jnp.where(slot <= token, inside, -jnp.inf))
    top = functools.reduce(jnp.maximum, [jnp.max(s, axis=1, keepdims=True) for s in scores])
    total = jnp.zeros((rows, 1), jnp.float32)
    mixed = jnp.zeros((rows, KV_RANK), jnp.float32)
    for row, s in enumerate(scores):
        weight = jnp.exp2((s - top) * EXP2_SCALE)
        total += jnp.sum(weight, axis=1, keepdims=True)
        values = keys[row, :, :KV_RANK] if row < ROWS else own_keys[:, :KV_RANK]
        mixed += jnp.dot(
            weight.astype(jnp.bfloat16), values, preferred_element_type=jnp.float32
        )
    latent = (mixed / total).astype(jnp.bfloat16)
    for head in range(q_even.shape[0]):
        out[:, head * VDIM : (head + 1) * VDIM] = jnp.dot(
            latent[head * QG : (head + 1) * QG], w_uv[head], preferred_element_type=jnp.float32
        ).astype(out.dtype)


def attend(q_even, q_odd, own, near, back, far, local, w_uv):
    heads = w_uv.shape[0]
    step = min(HEADS_STEP, heads)
    slots = RING * RING * SEL
    whole = lambda *shape: pl.BlockSpec(shape, lambda i: (0,) * len(shape))
    piece = whole(RING, SEL, own.shape[-1])
    queries = pl.BlockSpec((step, QG, KEY_WIDTH), lambda i: (i, 0, 0))
    keys = ROWS * slots + QG
    return pl.pallas_call(
        attend_kernel,
        grid=(heads // step,),
        in_specs=[queries, queries, piece, piece, piece, piece, whole(QG, KEY_WIDTH),
                  pl.BlockSpec((step, KV_RANK, VDIM), lambda i: (i, 0, 0))],
        out_specs=pl.BlockSpec((QG, step * VDIM), lambda i: (0, i)),
        out_shape=jax.ShapeDtypeStruct((QG, heads * VDIM), jnp.bfloat16),
        scratch_shapes=[
            pltpu.VMEM((ROWS, slots, KEY_WIDTH), jnp.bfloat16),
            pltpu.VMEM((QG, KEY_WIDTH), jnp.bfloat16),
        ],
        compiler_params=pltpu.CompilerParams(
            dimension_semantics=("arbitrary",), vmem_limit_bytes=40 * 1024 * 1024
        ),
        cost_estimate=pl.CostEstimate(
            flops=2 * heads * QG * keys * (KEY_WIDTH + KV_RANK),
            bytes_accessed=2 * (heads * QG * KEY_WIDTH * 2 + keys * KEY_WIDTH),
            transcendentals=heads * QG * keys,
        ),
        name="attend",
    )(q_even, q_odd, own, near, back, far, local, w_uv)


def project_kernel(heads, w_out, out):
    out[...] = jnp.dot(heads[...], w_out[...], preferred_element_type=jnp.float32).astype(out.dtype)


def project(heads, w_out, half):
    rows, depth = heads.shape
    columns = w_out.shape[1] // 2
    tiles = columns // OUT_TILE
    return pl.pallas_call(
        project_kernel,
        grid=(tiles,),
        in_specs=[
            pl.BlockSpec((rows, depth), lambda i: (0, 0)),
            pl.BlockSpec((depth, OUT_TILE), lambda i: (0, half * tiles + i)),
        ],
        out_specs=pl.BlockSpec((rows, OUT_TILE), lambda i: (0, i)),
        out_shape=jax.ShapeDtypeStruct((rows, columns), jnp.bfloat16),
        compiler_params=pltpu.CompilerParams(
            dimension_semantics=("arbitrary",), vmem_limit_bytes=16 * 1024 * 1024
        ),
        cost_estimate=pl.CostEstimate(
            flops=2 * rows * depth * columns,
            bytes_accessed=2 * depth * columns,
            transcendentals=0,
        ),
        name="project",
    )(heads, w_out)


def body(cache, span_latents, queries, selected, w_uv, w_out):
    seq_index = lax.axis_index("seq")
    mp_index = lax.axis_index("mp")
    y_index, core = seq_index // 2, seq_index % 2
    z_index, x_index = mp_index // RING, mp_index % RING
    blocks_here, block_rows, latent_width = cache.shape
    token_count = queries.shape[0]
    heads_here = w_uv.shape[0]
    groups_here = token_count // QG
    slots = groups_here * SEL

    requests = selected.reshape(RING, 2, slots) - seq_index * blocks_here
    requests = jnp.roll(requests, -y_index, axis=0)
    requests = jnp.where(core == 0, requests, requests[:, ::-1])
    picks = requests.transpose(1, 0, 2).reshape(-1)
    onehot = (picks[:, None] == lax.broadcasted_iota(jnp.int32, (1, blocks_here), 1)).astype(
        cache.dtype
    )
    flat = jnp.concatenate(
        [
            cache[:, :, :KV_RANK].reshape(blocks_here, block_rows * KV_RANK),
            cache[:, :, KV_RANK:].reshape(blocks_here, block_rows * ROPE),
        ],
        axis=1,
    )
    rows = jnp.dot(onehot, flat, preferred_element_type=jnp.float32).astype(cache.dtype)
    rows = rows.reshape(2, RING, slots, block_rows * latent_width)
    both = rows[0] + along_core(rows[1])
    shard = both[0] + along_y(both[1], 1) + along_y(both[2], 2) + along_y(both[3], 3)

    line = jnp.stack(
        [shard, along_plane(shard, True, 1), along_plane(shard, True, 3), along_plane(shard, True, 2)]
    )
    wide = queries.reshape(token_count, heads_here, latent_width).transpose(1, 0, 2)
    q_even = jnp.pad(wide, ((0, 0), (0, 0), (0, ROPE)))
    q_odd = jnp.concatenate(
        [wide[:, :, :KV_RANK], jnp.zeros_like(wide[:, :, KV_RANK:]), wide[:, :, KV_RANK:]], axis=2
    )
    local = jnp.pad(span_latents, ((0, 0), (0, ROPE)))
    lines = [line[:, g * SEL : (g + 1) * SEL] for g in range(groups_here)]
    planes = [[part] + [along_plane(part, False, step) for step in (1, 3, 2)] for part in lines]
    outputs = []
    for g in range(groups_here):
        at = slice(g * QG, (g + 1) * QG)
        outputs.append(attend(q_even[:, at], q_odd[:, at], *planes[g], local[at], w_uv))
    heads_all = jnp.concatenate(outputs, axis=0)

    own_rows = token_count // (RING * RING)
    first_index = jnp.where(core == 0, x_index, z_index)
    second_index = jnp.where(core == 0, z_index, x_index)
    near = heads_all.reshape(RING, RING, own_rows, heads_here * VDIM)
    near = jnp.where(core == 0, near.transpose(1, 0, 2, 3), near)
    near = jnp.roll(near, (-first_index, -second_index), axis=(0, 1))
    near = near.reshape(token_count, heads_here * VDIM)

    def scatter(value, first):
        parts = value.reshape(RING, value.shape[0] // RING, value.shape[1])
        total = parts[0].astype(jnp.float32)
        for step in (1, 3, 2):
            total = total + along_plane(parts[step], first, step).astype(jnp.float32)
        return total.astype(jnp.bfloat16)

    halves = [scatter(scatter(project(near, w_out, half), True), False) for half in range(2)]
    return jnp.concatenate(halves, axis=1)


def solution(mesh):
    return jax.shard_map(
        body,
        mesh=mesh,
        in_specs=(
            P("seq", "mp", None),
            P("seq", None),
            P("seq", "mp"),
            P(),
            P("mp", None, None),
            P("mp", None),
        ),
        out_specs=P(("seq", "mp"), None),
        check_vma=False,
    )
```

```python
import functools
import math

import jax
import jax.numpy as jnp
from jax import lax
from jax.experimental import pallas as pl
from jax.experimental.pallas import tpu as pltpu
from jax.sharding import PartitionSpec as P

KV_RANK = 512
ROPE = 64
VDIM = 128
QK_HEAD = 192
BLOCK = 64
SEL = 32
QG = 128
RING = 4
ROWS = 4
LAT = KV_RANK + ROPE
KEY_WIDTH = KV_RANK + 2 * ROPE
EXP2_SCALE = float(QK_HEAD) ** (-0.5) * math.log2(math.e)
HEADS_STEP = 4
OUT_TILE = 512


def index_of(y, core, z, x):
    return ((y * 2 + core) * RING + z) * RING + x


def pairs(move):
    out = []
    for y in range(RING):
        for core in range(2):
            for z in range(RING):
                for x in range(RING):
                    out.append((index_of(y, core, z, x), index_of(*move(y, core, z, x))))
    return out


def send(value, move):
    return lax.ppermute(value, ("seq", "mp"), pairs(move))


def along_core(value):
    return send(value, lambda y, core, z, x: (y, 1 - core, z, x))


def along_y(value, step):
    return send(value, lambda y, core, z, x: ((y + step) % RING, core, z, x))


def along_plane(value, first, step):
    def move(y, core, z, x):
        if (core == 0) == first:
            return y, core, z, (x + step) % RING
        return y, core, (z + step) % RING, x

    return send(value, move)


def attend_kernel(group, queries, own, near, back, far, local, w_uv, out, keys, own_keys, even, odd):
    for side, piece in enumerate((own, near, back, far)):
        for shard in range(RING):
            at = pl.ds((side * RING + shard) * SEL, SEL)
            for row in range(ROWS):
                rope = ROWS * KV_RANK + (row // 2) * 2 * ROPE
                keys[row, at, :KV_RANK] = piece[shard, :, row * KV_RANK : (row + 1) * KV_RANK]
                keys[row, at, KV_RANK:] = piece[shard, :, rope : rope + 2 * ROPE]
    mine = slice(group * QG, (group + 1) * QG)
    own_keys[:, :LAT] = local[mine, :]
    own_keys[:, LAT:] = jnp.zeros((QG, ROPE), own_keys.dtype)
    heads = w_uv.shape[0]
    zeros = jnp.zeros((QG, ROPE), even.dtype)
    for head in range(heads):
        at = slice(head * QG, (head + 1) * QG)
        latent = queries[mine, head * LAT : head * LAT + KV_RANK]
        rope = queries[mine, head * LAT + KV_RANK : (head + 1) * LAT]
        even[at, :KV_RANK] = latent
        odd[at, :KV_RANK] = latent
        even[at, KV_RANK:] = jnp.concatenate([rope, zeros], axis=1)
        odd[at, KV_RANK:] = jnp.concatenate([zeros, rope], axis=1)

    contract = (((1,), (1,)), ((), ()))
    rows = HEADS_STEP * QG
    for first in range(0, heads, HEADS_STEP):
        at = slice(first * QG, first * QG + rows)
        scores = [
            lax.dot_general(
                (even if row % 2 == 0 else odd)[at, :],
                keys[row],
                contract,
                preferred_element_type=jnp.float32,
            )
            for row in range(ROWS)
        ]
        inside = lax.dot_general(
            even[at, :], own_keys[...], contract, preferred_element_type=jnp.float32
        )
        token = lax.broadcasted_iota(jnp.int32, (rows, QG), 0) % QG
        slot = lax.broadcasted_iota(jnp.int32, (rows, QG), 1)
        scores.append(jnp.where(slot <= token, inside, -jnp.inf))
        top = functools.reduce(jnp.maximum, [jnp.max(s, axis=1, keepdims=True) for s in scores])
        total = jnp.zeros((rows, 1), jnp.float32)
        mixed = jnp.zeros((rows, KV_RANK), jnp.float32)
        for row, s in enumerate(scores):
            weight = jnp.exp2((s - top) * EXP2_SCALE)
            total += jnp.sum(weight, axis=1, keepdims=True)
            values = keys[row, :, :KV_RANK] if row < ROWS else own_keys[:, :KV_RANK]
            mixed += jnp.dot(
                weight.astype(jnp.bfloat16), values, preferred_element_type=jnp.float32
            )
        latent = (mixed / total).astype(jnp.bfloat16)
        for head in range(HEADS_STEP):
            out[:, (first + head) * VDIM : (first + head + 1) * VDIM] = jnp.dot(
                latent[head * QG : (head + 1) * QG],
                w_uv[first + head],
                preferred_element_type=jnp.float32,
            ).astype(out.dtype)


def attend(queries, pieces, local, w_uv, group):
    heads = w_uv.shape[0]
    slots = RING * RING * SEL
    keys = ROWS * slots + QG
    return pl.pallas_call(
        functools.partial(attend_kernel, group),
        in_specs=[pl.BlockSpec(memory_space=pltpu.VMEM)] * 7,
        out_specs=pl.BlockSpec(memory_space=pltpu.VMEM),
        out_shape=jax.ShapeDtypeStruct((QG, heads * VDIM), jnp.bfloat16),
        scratch_shapes=[
            pltpu.VMEM((ROWS, slots, KEY_WIDTH), jnp.bfloat16),
            pltpu.VMEM((QG, KEY_WIDTH), jnp.bfloat16),
            pltpu.VMEM((heads * QG, KEY_WIDTH), jnp.bfloat16),
            pltpu.VMEM((heads * QG, KEY_WIDTH), jnp.bfloat16),
        ],
        compiler_params=pltpu.CompilerParams(vmem_limit_bytes=24 * 1024 * 1024),
        cost_estimate=pl.CostEstimate(
            flops=2 * heads * QG * keys * (KEY_WIDTH + KV_RANK),
            bytes_accessed=2 * (heads * QG * KEY_WIDTH + keys * KEY_WIDTH),
            transcendentals=heads * QG * keys,
        ),
        name="attend",
    )(queries, *pieces, local, w_uv)


def project_kernel(half, heads, w_out, after, out):
    columns = w_out.shape[1] // 2
    for first in range(0, columns, OUT_TILE):
        out[:, first : first + OUT_TILE] = jnp.dot(
            heads[...],
            w_out[:, half * columns + first : half * columns + first + OUT_TILE],
            preferred_element_type=jnp.float32,
        ).astype(out.dtype)


def project(heads, w_out, after, half):
    rows, depth = heads.shape
    columns = w_out.shape[1] // 2
    return pl.pallas_call(
        functools.partial(project_kernel, half),
        in_specs=[
            pl.BlockSpec(memory_space=pltpu.VMEM),
            pl.BlockSpec(memory_space=pltpu.VMEM),
            pl.BlockSpec(memory_space=pl.ANY),
        ],
        out_specs=pl.BlockSpec(memory_space=pltpu.VMEM),
        out_shape=jax.ShapeDtypeStruct((rows, columns), jnp.bfloat16),
        compiler_params=pltpu.CompilerParams(vmem_limit_bytes=4 * 1024 * 1024),
        cost_estimate=pl.CostEstimate(
            flops=2 * rows * depth * columns,
            bytes_accessed=2 * depth * columns,
            transcendentals=0,
        ),
        name="project",
    )(heads, w_out, after)


def body(cache, span_latents, queries, selected, w_uv, w_out):
    seq_index = lax.axis_index("seq")
    mp_index = lax.axis_index("mp")
    y_index, core = seq_index // 2, seq_index % 2
    z_index, x_index = mp_index // RING, mp_index % RING
    blocks_here, block_rows, latent_width = cache.shape
    token_count = queries.shape[0]
    heads_here = w_uv.shape[0]
    groups_here = token_count // QG
    slots = groups_here * SEL

    requests = selected.reshape(RING, 2, slots) - seq_index * blocks_here
    requests = jnp.roll(requests, -y_index, axis=0)
    requests = jnp.where(core == 0, requests, requests[:, ::-1])
    flat = jnp.concatenate(
        [
            cache[:, :, :KV_RANK].reshape(blocks_here, block_rows * KV_RANK),
            cache[:, :, KV_RANK:].reshape(blocks_here, block_rows * ROPE),
        ],
        axis=1,
    )

    def collect(group):
        at = slice(group * SEL, (group + 1) * SEL)
        picks = requests[:, :, at].transpose(1, 0, 2).reshape(-1)
        onehot = (picks[:, None] == lax.broadcasted_iota(jnp.int32, (1, blocks_here), 1)).astype(
            cache.dtype
        )
        rows = jnp.dot(onehot, flat, preferred_element_type=jnp.float32).astype(cache.dtype)
        rows = rows.reshape(2, RING, SEL, block_rows * latent_width)
        both = rows[0] + along_core(rows[1])
        return both[0] + along_y(both[1], 1) + along_y(both[2], 2) + along_y(both[3], 3)

    shards = [collect(group) for group in range(groups_here)]
    lines = [
        jnp.stack([shard] + [along_plane(shard, True, step) for step in (1, 3, 2)])
        for shard in shards
    ]
    planes = [[line] + [along_plane(line, False, step) for step in (1, 3, 2)] for line in lines]
    outputs = [
        attend(queries, planes[g], span_latents, w_uv, g) for g in range(groups_here)
    ]
    heads_all = jnp.concatenate(outputs, axis=0)

    own_rows = token_count // (RING * RING)
    first_index = jnp.where(core == 0, x_index, z_index)
    second_index = jnp.where(core == 0, z_index, x_index)
    near = heads_all.reshape(RING, RING, own_rows, heads_here * VDIM)
    near = jnp.where(core == 0, near.transpose(1, 0, 2, 3), near)
    near = jnp.roll(near, (-first_index, -second_index), axis=(0, 1))
    near = near.reshape(token_count, heads_here * VDIM)

    def exchange(value, first):
        parts = value.reshape(RING, value.shape[0] // RING, value.shape[1])
        return [parts[0]] + [along_plane(parts[step], first, step) for step in (1, 3, 2)]

    def add(parts):
        total = functools.reduce(jnp.add, [part.astype(jnp.float32) for part in parts])
        return total.astype(jnp.bfloat16)

    after = near
    halves = []
    for half in range(2):
        received = exchange(project(near, w_out, after, half), True)
        after = received[1]
        halves.append(received)
    halves = [add(exchange(add(received), False)) for received in halves]
    return jnp.concatenate(halves, axis=1)


def solution(mesh):
    return jax.shard_map(
        body,
        mesh=mesh,
        in_specs=(
            P("seq", "mp", None),
            P("seq", None),
            P("seq", "mp"),
            P(),
            P("mp", None, None),
            P("mp", None),
        ),
        out_specs=P(("seq", "mp"), None),
        check_vma=False,
    )
```

```python
import functools
import math

import jax
import jax.numpy as jnp
from jax import lax
from jax.experimental import pallas as pl
from jax.experimental.pallas import tpu as pltpu
from jax.sharding import PartitionSpec as P

KV_RANK = 512
ROPE = 64
VDIM = 128
QK_HEAD = 192
BLOCK = 64
SEL = 32
QG = 128
RING = 4
ROWS = 4
LAT = KV_RANK + ROPE
KEY_WIDTH = KV_RANK + 2 * ROPE
EXP2_SCALE = float(QK_HEAD) ** (-0.5) * math.log2(math.e)
HEADS_STEP = 4
OUT_TILE = 512


def index_of(y, core, z, x):
    return ((y * 2 + core) * RING + z) * RING + x


def pairs(move):
    out = []
    for y in range(RING):
        for core in range(2):
            for z in range(RING):
                for x in range(RING):
                    out.append((index_of(y, core, z, x), index_of(*move(y, core, z, x))))
    return out


def send(value, move):
    return lax.ppermute(value, ("seq", "mp"), pairs(move))


def along_core(value):
    return send(value, lambda y, core, z, x: (y, 1 - core, z, x))


def along_y(value, step):
    return send(value, lambda y, core, z, x: ((y + step) % RING, core, z, x))


def along_plane(value, first, step):
    def move(y, core, z, x):
        if (core == 0) == first:
            return y, core, z, (x + step) % RING
        return y, core, (z + step) % RING, x

    return send(value, move)


CONTRACT = (((1,), (1,)), ((), ()))

def load_keys(pieces, keys):
    for row in range(ROWS):
        rope = ROWS * KV_RANK + (row // 2) * 2 * ROPE
        for side, piece in enumerate(pieces):
            shards = piece.shape[0]
            base = ((row // 2) * len(pieces) + side) * shards * SEL
            for shard in range(shards):
                at = pl.ds(base + shard * SEL, SEL)
                keys[row % 2, at, :KV_RANK] = piece[shard, :, row * KV_RANK : (row + 1) * KV_RANK]
                keys[row % 2, at, KV_RANK:] = piece[shard, :, rope : rope + 2 * ROPE]

def dot_keys(a, b):
    return lax.dot_general(a, b, CONTRACT, preferred_element_type=jnp.float32)

def weigh(scores, top):
    return [jnp.exp2((s - top) * EXP2_SCALE) for s in scores]

def first_kernel(group, queries, own, local, after, mixed, top, total, even, odd, passed, keys, own_keys):
    passed[...] = own[...]
    load_keys([own], keys)
    mine = slice(group * QG, (group + 1) * QG)
    own_keys[:, :LAT] = local[mine, :]
    own_keys[:, LAT:] = jnp.zeros((QG, ROPE), own_keys.dtype)
    heads = even.shape[0] // QG
    zeros = jnp.zeros((QG, ROPE), even.dtype)
    for head in range(heads):
        at = slice(head * QG, (head + 1) * QG)
        latent = queries[mine, head * LAT : head * LAT + KV_RANK]
        rope = queries[mine, head * LAT + KV_RANK : (head + 1) * LAT]
        even[at, :KV_RANK] = latent
        odd[at, :KV_RANK] = latent
        even[at, KV_RANK:] = jnp.concatenate([rope, zeros], axis=1)
        odd[at, KV_RANK:] = jnp.concatenate([zeros, rope], axis=1)
    rows = HEADS_STEP * QG
    for first in range(0, heads * QG, rows):
        at = slice(first, first + rows)
        inside = dot_keys(even[at, :], own_keys[...])
        token = lax.broadcasted_iota(jnp.int32, (rows, QG), 0) % QG
        slot = lax.broadcasted_iota(jnp.int32, (rows, QG), 1)
        scores = [
            dot_keys(even[at, :], keys[0]),
            dot_keys(odd[at, :], keys[1]),
            jnp.where(slot <= token, inside, -jnp.inf),
        ]
        high = functools.reduce(jnp.maximum, [jnp.max(s, axis=1, keepdims=True) for s in scores])
        weights = weigh(scores, high)
        top[at, :] = high
        total[at, :] = functools.reduce(jnp.add, [jnp.sum(w, axis=1, keepdims=True) for w in weights])
        values = [keys[0, :, :KV_RANK], keys[1, :, :KV_RANK], own_keys[:, :KV_RANK]]
        mixed[at, :] = jnp.dot(
            jnp.concatenate([w.astype(jnp.bfloat16) for w in weights], axis=1),
            jnp.concatenate(values, axis=0), preferred_element_type=jnp.float32)

def rest_kernel(mixed, top, total, even, odd, near, back, far, w_uv, out, keys):
    load_keys([near, back, far], keys)
    rows = HEADS_STEP * QG
    heads = w_uv.shape[0]
    for first in range(0, heads, HEADS_STEP):
        at = slice(first * QG, first * QG + rows)
        scores = [dot_keys(even[at, :], keys[0]), dot_keys(odd[at, :], keys[1])]
        before = top[at, :]
        high = functools.reduce(jnp.maximum, [before] + [jnp.max(s, axis=1, keepdims=True) for s in scores])
        weights = weigh(scores, high)
        kept = jnp.exp2((before - high) * EXP2_SCALE)
        count = kept * total[at, :] + functools.reduce(jnp.add, [jnp.sum(w, axis=1, keepdims=True) for w in weights])
        sums = jnp.dot(
            jnp.concatenate([w.astype(jnp.bfloat16) for w in weights], axis=1),
            jnp.concatenate([keys[0, :, :KV_RANK], keys[1, :, :KV_RANK]], axis=0), preferred_element_type=jnp.float32)
        latent = ((kept * mixed[at, :] + sums) / count).astype(jnp.bfloat16)
        for head in range(HEADS_STEP):
            out[:, (first + head) * VDIM : (first + head + 1) * VDIM] = jnp.dot(
                latent[head * QG : (head + 1) * QG], w_uv[first + head], preferred_element_type=jnp.float32
            ).astype(out.dtype)

def vmem(count):
    return [pl.BlockSpec(memory_space=pltpu.VMEM)] * count

def attend_first(queries, own, local, after, group):
    heads = queries.shape[1] // LAT
    r = heads * QG
    keys = RING * SEL * ROWS
    return pl.pallas_call(
        functools.partial(first_kernel, group),
        in_specs=vmem(3) + [pl.BlockSpec(memory_space=pl.ANY)],
        out_specs=vmem(6),
        out_shape=[jax.ShapeDtypeStruct((r, KV_RANK), jnp.float32), jax.ShapeDtypeStruct((r, 1), jnp.float32), jax.ShapeDtypeStruct((r, 1), jnp.float32),
          jax.ShapeDtypeStruct((r, KEY_WIDTH), jnp.bfloat16), jax.ShapeDtypeStruct((r, KEY_WIDTH), jnp.bfloat16),
          jax.ShapeDtypeStruct(own.shape, own.dtype)],
        scratch_shapes=[pltpu.VMEM((2, keys // 2, KEY_WIDTH), jnp.bfloat16), pltpu.VMEM((QG, KEY_WIDTH), jnp.bfloat16)],
        compiler_params=pltpu.CompilerParams(vmem_limit_bytes=10 * 1024 * 1024),
        cost_estimate=pl.CostEstimate(flops=2 * r * (keys + QG) * (KEY_WIDTH + KV_RANK), bytes_accessed=2 * r * KEY_WIDTH, transcendentals=r * (keys + QG)),
        name="attend_own",
    )(queries, own, local, after)

def attend_rest(state, pieces, w_uv):
    heads = w_uv.shape[0]
    r = heads * QG
    keys = 3 * RING * SEL * ROWS
    return pl.pallas_call(
        rest_kernel,
        in_specs=vmem(9), out_specs=pl.BlockSpec(memory_space=pltpu.VMEM),
        out_shape=jax.ShapeDtypeStruct((QG, heads * VDIM), jnp.bfloat16),
        scratch_shapes=[pltpu.VMEM((2, keys // 2, KEY_WIDTH), jnp.bfloat16)],
        compiler_params=pltpu.CompilerParams(vmem_limit_bytes=14 * 1024 * 1024),
        cost_estimate=pl.CostEstimate(flops=2 * r * keys * (KEY_WIDTH + KV_RANK), bytes_accessed=2 * r * KEY_WIDTH, transcendentals=r * keys),
        name="attend_rest",
    )(*state, *pieces, w_uv)


def project_kernel(heads, w_out, out):
    for first in range(0, w_out.shape[1], OUT_TILE):
        at = slice(first, first + OUT_TILE)
        out[:, at] = jnp.dot(
            heads[...], w_out[:, at], preferred_element_type=jnp.float32
        ).astype(out.dtype)


def project(heads, w_out):
    rows, depth = heads.shape
    columns = w_out.shape[1]
    return pl.pallas_call(
        project_kernel,
        in_specs=vmem(2),
        out_specs=pl.BlockSpec(memory_space=pltpu.VMEM),
        out_shape=jax.ShapeDtypeStruct((rows, columns), jnp.bfloat16),
        compiler_params=pltpu.CompilerParams(vmem_limit_bytes=4 * 1024 * 1024),
        cost_estimate=pl.CostEstimate(
            flops=2 * rows * depth * columns,
            bytes_accessed=2 * depth * columns,
            transcendentals=0,
        ),
        name="project",
    )(heads, w_out)


def body(cache, span_latents, queries, selected, w_uv, w_out):
    seq_index = lax.axis_index("seq")
    mp_index = lax.axis_index("mp")
    y_index, core = seq_index // 2, seq_index % 2
    z_index, x_index = mp_index // RING, mp_index % RING
    blocks_here, block_rows, latent_width = cache.shape
    token_count = queries.shape[0]
    heads_here = w_uv.shape[0]
    groups_here = token_count // QG
    slots = groups_here * SEL

    requests = selected.reshape(RING, 2, slots) - seq_index * blocks_here
    requests = jnp.roll(requests, -y_index, axis=0)
    requests = jnp.where(core == 0, requests, requests[:, ::-1])
    flat = jnp.concatenate(
        [
            cache[:, :, :KV_RANK].reshape(blocks_here, block_rows * KV_RANK),
            cache[:, :, KV_RANK:].reshape(blocks_here, block_rows * ROPE),
        ],
        axis=1,
    )

    picks = requests.transpose(1, 0, 2).reshape(-1)
    onehot = (picks[:, None] == lax.broadcasted_iota(jnp.int32, (1, blocks_here), 1)).astype(
        cache.dtype
    )
    rows = jnp.dot(onehot, flat, preferred_element_type=jnp.float32).astype(cache.dtype)
    rows = rows.reshape(2, RING, slots, block_rows * latent_width)
    both = rows[0] + along_core(rows[1])
    shard = both[0] + along_y(both[1], 1) + along_y(both[3], 3) + along_y(both[2], 2)

    line = jnp.stack([shard] + [along_plane(shard, True, step) for step in (1, 3, 2)])
    lines = [line[:, g * SEL : (g + 1) * SEL] for g in range(groups_here)]
    states = []
    planes = []
    passed = line
    for g, part in enumerate(lines):
        *state, passed = attend_first(queries, part, span_latents, passed, g)
        states.append(state)
        last = passed if g == groups_here - 1 else part
        planes.append([along_plane(p, False, step) for p, step in ((part, 1), (part, 3), (last, 2))])
    outputs = [attend_rest(states[g], planes[g], w_uv) for g in range(groups_here)]
    heads_all = jnp.concatenate(outputs, axis=0)

    own_rows = token_count // (RING * RING)
    first_index = jnp.where(core == 0, x_index, z_index)
    second_index = jnp.where(core == 0, z_index, x_index)
    near = heads_all.reshape(RING, RING, own_rows, heads_here * VDIM)
    near = jnp.where(core == 0, near.transpose(1, 0, 2, 3), near)
    near = jnp.roll(near, (-first_index, -second_index), axis=(0, 1))
    near = near.reshape(token_count, heads_here * VDIM)

    def scatter(value, first):
        parts = value.reshape(RING, value.shape[0] // RING, value.shape[1])
        parts = [parts[0]] + [along_plane(parts[step], first, step) for step in (1, 3, 2)]
        total = functools.reduce(jnp.add, [part.astype(jnp.float32) for part in parts])
        return total.astype(jnp.bfloat16)

    return scatter(scatter(project(near, w_out), True), False)


def solution(mesh):
    return jax.shard_map(
        body,
        mesh=mesh,
        in_specs=(
            P("seq", "mp", None),
            P("seq", None),
            P("seq", "mp"),
            P(),
            P("mp", None, None),
            P("mp", None),
        ),
        out_specs=P(("seq", "mp"), None),
        check_vma=False,
    )
```

```python
import functools
import math

import jax
import jax.numpy as jnp
import numpy as np
from jax import lax
from jax.experimental import pallas as pl
from jax.experimental.pallas import tpu as pltpu
from jax.sharding import PartitionSpec as P

KV_RANK = 512
ROPE = 64
VDIM = 128
QK_HEAD = 192
BLOCK = 64
SEL = 32
QG = 128
RING = 4
ROWS = 4
LAT = KV_RANK + ROPE
KEY_WIDTH = KV_RANK + 2 * ROPE
EXP2_SCALE = float(QK_HEAD) ** (-0.5) * math.log2(math.e)
HEADS_STEP = 4
OUT_TILE = 512
WHOLE_LIMIT = 16
FIRST_LIMIT = 10
REST_LIMIT = 14


def index_of(y, core, z, x):
    return ((y * 2 + core) * RING + z) * RING + x


def pairs(move):
    out = []
    for y in range(RING):
        for core in range(2):
            for z in range(RING):
                for x in range(RING):
                    out.append((index_of(y, core, z, x), index_of(*move(y, core, z, x))))
    return out


def send(value, move):
    return lax.ppermute(value, ("seq", "mp"), pairs(move))


def along_core(value):
    return send(value, lambda y, core, z, x: (y, 1 - core, z, x))


def along_y(value, step):
    return send(value, lambda y, core, z, x: ((y + step) % RING, core, z, x))


def along_plane(value, first, step):
    def move(y, core, z, x):
        if (core == 0) == first:
            return y, core, z, (x + step) % RING
        return y, core, (z + step) % RING, x

    return send(value, move)


CONTRACT = (((1,), (1,)), ((), ()))

def load_keys(pieces, keys):
    for row in range(ROWS):
        rope = ROWS * KV_RANK + (row // 2) * 2 * ROPE
        base = row // 2 * (keys.shape[1] // 2)
        for piece in pieces:
            for shard in range(piece.shape[0]):
                at = pl.ds(base, SEL)
                keys[row % 2, at, :KV_RANK] = piece[shard, :, row * KV_RANK : (row + 1) * KV_RANK]
                keys[row % 2, at, KV_RANK:] = piece[shard, :, rope : rope + 2 * ROPE]
                base += SEL


def load_own(local, own_keys, mine):
    own_keys[:, :LAT] = local[:, mine].T
    own_keys[:, LAT:] = jnp.zeros((QG, ROPE), own_keys.dtype)


def load_queries(queries, even, odd, mine):
    zeros = jnp.zeros((QG, ROPE), even.dtype)
    for head in range(even.shape[0] // QG):
        at = slice(head * QG, (head + 1) * QG)
        latent = queries[mine, head * LAT : head * LAT + KV_RANK]
        rope = queries[mine, head * LAT + KV_RANK : (head + 1) * LAT]
        even[at, :KV_RANK] = latent
        odd[at, :KV_RANK] = latent
        even[at, KV_RANK:] = jnp.concatenate([rope, zeros], axis=1)
        odd[at, KV_RANK:] = jnp.concatenate([zeros, rope], axis=1)


def dot_keys(a, b):
    return lax.dot_general(a, b, CONTRACT, preferred_element_type=jnp.float32)


def inside(queries, own_keys):
    scores = dot_keys(queries, own_keys[...])
    token = lax.broadcasted_iota(jnp.int32, scores.shape, 0) % QG
    slot = lax.broadcasted_iota(jnp.int32, scores.shape, 1)
    return jnp.where(slot <= token, scores, -jnp.inf)


def highest(values):
    return functools.reduce(jnp.maximum, [jnp.max(v, axis=1, keepdims=True) for v in values])


def weigh(scores, high):
    return [jnp.exp2((s - high) * EXP2_SCALE) for s in scores]


def count(weights):
    return functools.reduce(jnp.add, [jnp.sum(w, axis=1, keepdims=True) for w in weights])


def mix(weights, values):
    return jnp.dot(
        jnp.concatenate([w.astype(jnp.bfloat16) for w in weights], axis=1),
        jnp.concatenate(values, axis=0),
        preferred_element_type=jnp.float32,
    )


def raise_values(latent, w_uv, out, first):
    for head in range(HEADS_STEP):
        out[:, (first + head) * VDIM : (first + head + 1) * VDIM] = jnp.dot(
            latent[head * QG : (head + 1) * QG],
            w_uv[first + head],
            preferred_element_type=jnp.float32,
        ).astype(out.dtype)


def whole_kernel(group, queries, *refs):
    *pieces, local, w_uv, out, keys, own_keys, even, odd = refs
    mine = slice(group * QG, (group + 1) * QG)
    load_keys(pieces, keys)
    load_own(local, own_keys, mine)
    load_queries(queries, even, odd, mine)
    for first in range(0, w_uv.shape[0], HEADS_STEP):
        at = slice(first * QG, (first + HEADS_STEP) * QG)
        scores = [
            dot_keys(even[at, :], keys[0]),
            dot_keys(odd[at, :], keys[1]),
            inside(even[at, :], own_keys),
        ]
        weights = weigh(scores, highest(scores))
        values = [keys[0, :, :KV_RANK], keys[1, :, :KV_RANK], own_keys[:, :KV_RANK]]
        latent = (mix(weights, values) / count(weights)).astype(jnp.bfloat16)
        raise_values(latent, w_uv, out, first)


def first_kernel(group, queries, own, local, mixed, state, passed, keys, own_keys, even, odd):
    passed[...] = own[...]
    mine = slice(group * QG, (group + 1) * QG)
    load_keys([own], keys)
    load_own(local, own_keys, mine)
    load_queries(queries, even, odd, mine)
    rows = HEADS_STEP * QG
    for first in range(0, even.shape[0], rows):
        at = slice(first, first + rows)
        scores = [
            dot_keys(even[at, :], keys[0]),
            dot_keys(odd[at, :], keys[1]),
            inside(even[at, :], own_keys),
        ]
        high = highest(scores)
        weights = weigh(scores, high)
        values = [keys[0, :, :KV_RANK], keys[1, :, :KV_RANK], own_keys[:, :KV_RANK]]
        state[at, 0:1] = high
        state[at, 1:2] = count(weights)
        mixed[at, :] = mix(weights, values)


def rest_kernel(group, queries, mixed, state, *refs):
    *pieces, w_uv, out, keys, even, odd = refs
    load_keys(pieces, keys)
    load_queries(queries, even, odd, slice(group * QG, (group + 1) * QG))
    for first in range(0, w_uv.shape[0], HEADS_STEP):
        at = slice(first * QG, (first + HEADS_STEP) * QG)
        scores = [dot_keys(even[at, :], keys[0]), dot_keys(odd[at, :], keys[1])]
        before = state[at, 0:1]
        high = jnp.maximum(before, highest(scores))
        weights = weigh(scores, high)
        kept = jnp.exp2((before - high) * EXP2_SCALE)
        total = kept * state[at, 1:2] + count(weights)
        sums = mix(weights, [keys[0, :, :KV_RANK], keys[1, :, :KV_RANK]])
        latent = ((kept * mixed[at, :] + sums) / total).astype(jnp.bfloat16)
        raise_values(latent, w_uv, out, first)


def vmem(number):
    return [pl.BlockSpec(memory_space=pltpu.VMEM)] * number


def attend_call(kernel, name, operands, out_shape, prior, own, rows, limit):
    keys = prior + own
    scratch = [pltpu.VMEM((2, prior // 2, KEY_WIDTH), jnp.bfloat16)]
    scratch += [pltpu.VMEM((own, KEY_WIDTH), jnp.bfloat16)] * (own > 0)
    scratch += [pltpu.VMEM((rows, KEY_WIDTH), jnp.bfloat16)] * 2
    return pl.pallas_call(
        kernel,
        in_specs=vmem(len(operands)),
        out_specs=vmem(len(out_shape)),
        out_shape=out_shape,
        scratch_shapes=scratch,
        compiler_params=pltpu.CompilerParams(vmem_limit_bytes=limit * 1024 * 1024),
        cost_estimate=pl.CostEstimate(
            flops=2 * rows * keys * (KEY_WIDTH + KV_RANK),
            bytes_accessed=2 * (rows + keys) * KEY_WIDTH,
            transcendentals=rows * keys,
        ),
        name=name,
    )(*operands)


def attend_whole(queries, pieces, local, w_uv, group):
    heads = w_uv.shape[0]
    return attend_call(
        functools.partial(whole_kernel, group),
        "attend_whole",
        (queries, *pieces, local, w_uv),
        [jax.ShapeDtypeStruct((QG, heads * VDIM), jnp.bfloat16)],
        RING * RING * SEL * ROWS,
        QG,
        heads * QG,
        WHOLE_LIMIT,
    )[0]


def attend_first(queries, own, local, group):
    rows = queries.shape[1] // LAT * QG
    return attend_call(
        functools.partial(first_kernel, group),
        "attend_first",
        (queries, own, local),
        [
            jax.ShapeDtypeStruct((rows, KV_RANK), jnp.float32),
            jax.ShapeDtypeStruct((rows, 2), jnp.float32),
            jax.ShapeDtypeStruct(own.shape, own.dtype),
        ],
        RING * SEL * ROWS,
        QG,
        rows,
        FIRST_LIMIT,
    )


def attend_rest(queries, mixed, state, pieces, w_uv, group):
    heads = w_uv.shape[0]
    return attend_call(
        functools.partial(rest_kernel, group),
        "attend_rest",
        (queries, mixed, state, *pieces, w_uv),
        [jax.ShapeDtypeStruct((QG, heads * VDIM), jnp.bfloat16)],
        3 * RING * SEL * ROWS,
        0,
        heads * QG,
        REST_LIMIT,
    )[0]


def project_kernel(groups, order, *refs):
    heads, w_out, chunks, (given, near) = (
        refs[:groups],
        refs[groups],
        refs[groups + 1 : groups + 1 + RING],
        refs[groups + 1 + RING :],
    )
    for g, part in enumerate(heads):
        given[g * QG : (g + 1) * QG, :] = part[...]
    blocks = RING * RING
    own_rows = groups * QG // blocks
    for block in range(blocks):
        at = pl.ds(pl.multiple_of(order[block] * own_rows, own_rows), own_rows)
        near[block * own_rows : (block + 1) * own_rows, :] = given[at, :]
    rows = RING * own_rows
    for first in range(0, w_out.shape[1], OUT_TILE):
        at = slice(first, first + OUT_TILE)
        terms = jnp.dot(near[...], w_out[:, at], preferred_element_type=jnp.float32)
        for step, chunk in enumerate(chunks):
            chunk[:, at] = terms[step * rows : (step + 1) * rows].astype(chunk.dtype)


def project(order, heads, w_out):
    groups = len(heads)
    rows, depth = groups * QG, w_out.shape[0]
    columns = w_out.shape[1]
    return pl.pallas_call(
        functools.partial(project_kernel, groups),
        in_specs=[pl.BlockSpec(memory_space=pltpu.SMEM)] + vmem(groups + 1),
        out_specs=vmem(RING),
        out_shape=[jax.ShapeDtypeStruct((rows // RING, columns), jnp.bfloat16)] * RING,
        scratch_shapes=[pltpu.VMEM((rows, depth), jnp.bfloat16)] * 2,
        compiler_params=pltpu.CompilerParams(vmem_limit_bytes=6 * 1024 * 1024),
        cost_estimate=pl.CostEstimate(
            flops=2 * rows * depth * columns,
            bytes_accessed=2 * depth * columns,
            transcendentals=0,
        ),
        name="project",
    )(order, *heads, w_out)


def block_orders():
    orders = np.zeros((2, RING, RING, RING, RING), np.int32)
    for core, z, x, one, two in np.ndindex(*orders.shape):
        if core == 0:
            orders[core, z, x, one, two] = (z + two) % RING * RING + (x + one) % RING
        else:
            orders[core, z, x, one, two] = (z + one) % RING * RING + (x + two) % RING
    return orders.reshape(2 * RING * RING, RING * RING)


def body(cache, span_latents, queries, selected, w_uv, w_out):
    seq_index = lax.axis_index("seq")
    mp_index = lax.axis_index("mp")
    y_index, core = seq_index // 2, seq_index % 2
    blocks_here, block_rows, latent_width = cache.shape
    token_count = queries.shape[0]
    groups_here = token_count // QG
    slots = groups_here * SEL

    order = lax.dynamic_index_in_dim(
        jnp.asarray(block_orders()), core * RING * RING + mp_index, 0, keepdims=False
    )
    selected, order = lax.optimization_barrier((selected, order))
    requests = selected.reshape(RING, 2, slots) - seq_index * blocks_here
    requests = jnp.roll(requests, -y_index, axis=0)
    requests = jnp.where(core == 0, requests, requests[:, ::-1])
    flat = jnp.concatenate(
        [
            cache[:, :, :KV_RANK].reshape(blocks_here, block_rows * KV_RANK),
            cache[:, :, KV_RANK:].reshape(blocks_here, block_rows * ROPE),
        ],
        axis=1,
    )

    picks = requests.transpose(1, 0, 2).reshape(-1)
    onehot = (picks[:, None] == lax.broadcasted_iota(jnp.int32, (1, blocks_here), 1)).astype(
        cache.dtype
    )
    rows = jnp.dot(onehot, flat, preferred_element_type=jnp.float32).astype(cache.dtype)
    rows = rows.reshape(2, RING, slots, block_rows * latent_width)
    both = rows[0] + along_core(rows[1])
    shard = both[0] + along_y(both[1], 1) + along_y(both[3], 3) + along_y(both[2], 2)

    line = jnp.stack([shard] + [along_plane(shard, True, step) for step in (1, 3, 2)])
    lines = [line[:, g * SEL : (g + 1) * SEL] for g in range(groups_here)]
    local = span_latents.T
    last = groups_here - 1
    mixed, state, passed = attend_first(queries, lines[last], local, last)
    planes = [[along_plane(part, False, step) for step in (1, 3)] for part in lines]
    half = RING // 2
    for plane in planes:
        plane.append(along_plane(plane[0][:half], False, 1))
        plane.append(along_plane(plane[1][half:], False, 3))
    outputs = [
        attend_whole(queries, [lines[g]] + planes[g], local, w_uv, g) for g in range(last)
    ]
    outputs.append(attend_rest(queries, mixed, state, planes[last], w_uv, last))

    def scatter(parts, first):
        parts = [parts[0]] + [along_plane(parts[step], first, step) for step in (1, 3, 2)]
        total = functools.reduce(jnp.add, [part.astype(jnp.float32) for part in parts])
        return total.astype(jnp.bfloat16)

    total = scatter(project(order, outputs, w_out), True)
    return scatter(total.reshape(RING, total.shape[0] // RING, total.shape[1]), False)


def solution(mesh):
    return jax.shard_map(
        body,
        mesh=mesh,
        in_specs=(
            P("seq", "mp", None),
            P("seq", None),
            P("seq", "mp"),
            P(),
            P("mp", None, None),
            P("mp", None),
        ),
        out_specs=P(("seq", "mp"), None),
        check_vma=False,
    )
```

```python
import functools
import math

import jax
import jax.numpy as jnp
import numpy as np
from jax import lax
from jax.experimental import pallas as pl
from jax.experimental.pallas import tpu as pltpu
from jax.sharding import PartitionSpec as P

KV_RANK = 512
ROPE = 64
VDIM = 128
QK_HEAD = 192
BLOCK = 64
SEL = 32
QG = 128
RING = 4
ROWS = 4
LAT = KV_RANK + ROPE
KEY_WIDTH = KV_RANK + 2 * ROPE
EXP2_SCALE = float(QK_HEAD) ** (-0.5) * math.log2(math.e)
HEADS_STEP = 4
OUT_TILE = 512
FIRST_LIMIT = 10
REST_LIMIT = 14


def index_of(y, core, z, x):
    return ((y * 2 + core) * RING + z) * RING + x


def pairs(move):
    out = []
    for y in range(RING):
        for core in range(2):
            for z in range(RING):
                for x in range(RING):
                    out.append((index_of(y, core, z, x), index_of(*move(y, core, z, x))))
    return out


def send(value, move):
    return lax.ppermute(value, ("seq", "mp"), pairs(move))


def along_core(value):
    return send(value, lambda y, core, z, x: (y, 1 - core, z, x))


def along_y(value, step):
    return send(value, lambda y, core, z, x: ((y + step) % RING, core, z, x))


def along_plane(value, first, step):
    def move(y, core, z, x):
        if (core == 0) == first:
            return y, core, z, (x + step) % RING
        return y, core, (z + step) % RING, x

    return send(value, move)


CONTRACT = (((1,), (1,)), ((), ()))

def load_keys(pieces, keys):
    for row in range(ROWS):
        rope = ROWS * KV_RANK + (row // 2) * 2 * ROPE
        base = row // 2 * (keys.shape[1] // 2)
        for piece in pieces:
            for shard in range(piece.shape[0]):
                at = pl.ds(base, SEL)
                keys[row % 2, at, :KV_RANK] = piece[shard, :, row * KV_RANK : (row + 1) * KV_RANK]
                keys[row % 2, at, KV_RANK:] = piece[shard, :, rope : rope + 2 * ROPE]
                base += SEL


def load_own(local, own_keys, mine):
    own_keys[:, :LAT] = local[:, mine].T
    own_keys[:, LAT:] = jnp.zeros((QG, ROPE), own_keys.dtype)


def load_queries(queries, even, odd, mine):
    zeros = jnp.zeros((QG, ROPE), even.dtype)
    for head in range(even.shape[0] // QG):
        at = slice(head * QG, (head + 1) * QG)
        latent = queries[mine, head * LAT : head * LAT + KV_RANK]
        rope = queries[mine, head * LAT + KV_RANK : (head + 1) * LAT]
        even[at, :KV_RANK] = latent
        odd[at, :KV_RANK] = latent
        even[at, KV_RANK:] = jnp.concatenate([rope, zeros], axis=1)
        odd[at, KV_RANK:] = jnp.concatenate([zeros, rope], axis=1)


def dot_keys(a, b):
    return lax.dot_general(a, b, CONTRACT, preferred_element_type=jnp.float32)


def inside(queries, own_keys):
    scores = dot_keys(queries, own_keys[...])
    token = lax.broadcasted_iota(jnp.int32, scores.shape, 0) % QG
    slot = lax.broadcasted_iota(jnp.int32, scores.shape, 1)
    return jnp.where(slot <= token, scores, -jnp.inf)


def highest(values):
    return functools.reduce(jnp.maximum, [jnp.max(v, axis=1, keepdims=True) for v in values])


def weigh(scores, high):
    return [jnp.exp2((s - high) * EXP2_SCALE) for s in scores]


def count(weights):
    return functools.reduce(jnp.add, [jnp.sum(w, axis=1, keepdims=True) for w in weights])


def mix(weights, values):
    return jnp.dot(
        jnp.concatenate([w.astype(jnp.bfloat16) for w in weights], axis=1),
        jnp.concatenate(values, axis=0),
        preferred_element_type=jnp.float32,
    )


def raise_values(latent, w_uv, out, first):
    for head in range(HEADS_STEP):
        out[:, (first + head) * VDIM : (first + head + 1) * VDIM] = jnp.dot(
            latent[head * QG : (head + 1) * QG],
            w_uv[first + head],
            preferred_element_type=jnp.float32,
        ).astype(out.dtype)


def first_kernel(group, queries, own, local, mixed, state, keys, own_keys, even, odd):
    mine = slice(group * QG, (group + 1) * QG)
    load_keys([own], keys)
    load_own(local, own_keys, mine)
    load_queries(queries, even, odd, mine)
    rows = HEADS_STEP * QG
    for first in range(0, even.shape[0], rows):
        at = slice(first, first + rows)
        scores = [
            dot_keys(even[at, :], keys[0]),
            dot_keys(odd[at, :], keys[1]),
            inside(even[at, :], own_keys),
        ]
        high = highest(scores)
        weights = weigh(scores, high)
        values = [keys[0, :, :KV_RANK], keys[1, :, :KV_RANK], own_keys[:, :KV_RANK]]
        state[at, 0:1] = high
        state[at, 1:2] = count(weights)
        mixed[at, :] = mix(weights, values)


def rest_kernel(group, queries, mixed, state, *refs):
    *pieces, w_uv, out, keys, even, odd = refs
    load_keys(pieces, keys)
    load_queries(queries, even, odd, slice(group * QG, (group + 1) * QG))
    for first in range(0, w_uv.shape[0], HEADS_STEP):
        at = slice(first * QG, (first + HEADS_STEP) * QG)
        scores = [dot_keys(even[at, :], keys[0]), dot_keys(odd[at, :], keys[1])]
        before = state[at, 0:1]
        high = jnp.maximum(before, highest(scores))
        weights = weigh(scores, high)
        kept = jnp.exp2((before - high) * EXP2_SCALE)
        total = kept * state[at, 1:2] + count(weights)
        sums = mix(weights, [keys[0, :, :KV_RANK], keys[1, :, :KV_RANK]])
        latent = ((kept * mixed[at, :] + sums) / total).astype(jnp.bfloat16)
        raise_values(latent, w_uv, out, first)


def vmem(number):
    return [pl.BlockSpec(memory_space=pltpu.VMEM)] * number


def attend_call(kernel, name, operands, out_shape, prior, own, rows, limit):
    keys = prior + own
    scratch = [pltpu.VMEM((2, prior // 2, KEY_WIDTH), jnp.bfloat16)]
    scratch += [pltpu.VMEM((own, KEY_WIDTH), jnp.bfloat16)] * (own > 0)
    scratch += [pltpu.VMEM((rows, KEY_WIDTH), jnp.bfloat16)] * 2
    return pl.pallas_call(
        kernel,
        in_specs=vmem(len(operands)),
        out_specs=vmem(len(out_shape)),
        out_shape=out_shape,
        scratch_shapes=scratch,
        compiler_params=pltpu.CompilerParams(vmem_limit_bytes=limit * 1024 * 1024),
        cost_estimate=pl.CostEstimate(
            flops=2 * rows * keys * (KEY_WIDTH + KV_RANK),
            bytes_accessed=2 * (rows + keys) * KEY_WIDTH,
            transcendentals=rows * keys,
        ),
        name=name,
    )(*operands)


def attend_first(queries, own, local, group):
    rows = queries.shape[1] // LAT * QG
    return attend_call(
        functools.partial(first_kernel, group),
        "attend_first",
        (queries, own, local),
        [
            jax.ShapeDtypeStruct((rows, KV_RANK), jnp.float32),
            jax.ShapeDtypeStruct((rows, 2), jnp.float32),
        ],
        RING * SEL * ROWS,
        QG,
        rows,
        FIRST_LIMIT,
    )


def attend_rest(queries, mixed, state, pieces, w_uv, group):
    heads = w_uv.shape[0]
    return attend_call(
        functools.partial(rest_kernel, group),
        "attend_rest",
        (queries, mixed, state, *pieces, w_uv),
        [jax.ShapeDtypeStruct((QG, heads * VDIM), jnp.bfloat16)],
        3 * RING * SEL * ROWS,
        0,
        heads * QG,
        REST_LIMIT,
    )[0]


def halves_kernel(up, down, *refs):
    *_, low, high = refs
    half = up.shape[0] // 2
    low[...] = up[:half]
    high[...] = down[half:]


def halves(up, down, after):
    shape = jax.ShapeDtypeStruct((up.shape[0] // 2,) + up.shape[1:], up.dtype)
    return pl.pallas_call(
        halves_kernel,
        in_specs=vmem(2) + [pl.BlockSpec(memory_space=pl.ANY)] * len(after),
        out_specs=vmem(2),
        out_shape=[shape] * 2,
        compiler_params=pltpu.CompilerParams(vmem_limit_bytes=1024 * 1024),
        cost_estimate=pl.CostEstimate(flops=0, bytes_accessed=0, transcendentals=0),
        name="halves",
    )(up, down, *after)


def project_kernel(groups, blocks, tokens, order, *refs):
    heads, w_out = refs[:groups], refs[groups]
    chunks, (given, near) = refs[groups + 1 + tokens : -2], refs[-2:]
    for g, part in enumerate(heads):
        given[g * QG : (g + 1) * QG, :] = part[...]
    own_rows = given.shape[0] // (RING * RING)
    for at, block in enumerate(blocks):
        start = pl.ds(pl.multiple_of(order[block] * own_rows, own_rows), own_rows)
        near[at * own_rows : (at + 1) * own_rows, :] = given[start, :]
    rows = chunks[0].shape[0]
    for first in range(0, w_out.shape[1], OUT_TILE):
        at = slice(first, first + OUT_TILE)
        terms = jnp.dot(near[...], w_out[:, at], preferred_element_type=jnp.float32)
        for step, chunk in enumerate(chunks):
            chunk[:, at] = terms[step * rows : (step + 1) * rows].astype(chunk.dtype)


def project(order, heads, w_out, blocks, pieces, after):
    groups = len(heads)
    depth, columns = w_out.shape
    rows = len(blocks) * (groups * QG // (RING * RING))
    return pl.pallas_call(
        functools.partial(project_kernel, groups, blocks, len(after)),
        in_specs=[pl.BlockSpec(memory_space=pltpu.SMEM)]
        + vmem(groups + 1)
        + [pl.BlockSpec(memory_space=pl.ANY)] * len(after),
        out_specs=vmem(pieces),
        out_shape=[jax.ShapeDtypeStruct((rows // pieces, columns), jnp.bfloat16)] * pieces,
        scratch_shapes=[
            pltpu.VMEM((groups * QG, depth), jnp.bfloat16),
            pltpu.VMEM((rows, depth), jnp.bfloat16),
        ],
        compiler_params=pltpu.CompilerParams(vmem_limit_bytes=6 * 1024 * 1024),
        cost_estimate=pl.CostEstimate(
            flops=2 * rows * depth * columns,
            bytes_accessed=2 * depth * columns,
            transcendentals=0,
        ),
        name="project",
    )(order, *heads, w_out, *after)


def block_orders():
    orders = np.zeros((2, RING, RING, RING, RING), np.int32)
    for core, z, x, one, two in np.ndindex(*orders.shape):
        if core == 0:
            orders[core, z, x, one, two] = (z + two) % RING * RING + (x + one) % RING
        else:
            orders[core, z, x, one, two] = (z + one) % RING * RING + (x + two) % RING
    return orders.reshape(2 * RING * RING, RING * RING)


def body(cache, span_latents, queries, selected, w_uv, w_out):
    seq_index = lax.axis_index("seq")
    mp_index = lax.axis_index("mp")
    y_index, core = seq_index // 2, seq_index % 2
    blocks_here, block_rows, latent_width = cache.shape
    token_count = queries.shape[0]
    groups_here = token_count // QG
    slots = groups_here * SEL

    order = lax.dynamic_index_in_dim(
        jnp.asarray(block_orders()), core * RING * RING + mp_index, 0, keepdims=False
    )
    selected, order = lax.optimization_barrier((selected, order))
    requests = selected.reshape(RING, 2, slots) - seq_index * blocks_here
    requests = jnp.roll(requests, -y_index, axis=0)
    requests = jnp.where(core == 0, requests, requests[:, ::-1])
    flat = jnp.concatenate(
        [
            cache[:, :, :KV_RANK].reshape(blocks_here, block_rows * KV_RANK),
            cache[:, :, KV_RANK:].reshape(blocks_here, block_rows * ROPE),
        ],
        axis=1,
    )

    picks = requests.transpose(1, 0, 2).reshape(-1)
    onehot = (picks[:, None] == lax.broadcasted_iota(jnp.int32, (1, blocks_here), 1)).astype(
        cache.dtype
    )
    rows = jnp.dot(onehot, flat, preferred_element_type=jnp.float32).astype(cache.dtype)
    rows = rows.reshape(2, RING, slots, block_rows * latent_width)
    both = rows[0] + along_core(rows[1])
    shard = both[0] + along_y(both[1], 1) + along_y(both[3], 3) + along_y(both[2], 2)

    line = jnp.stack([shard] + [along_plane(shard, True, step) for step in (1, 3, 2)])
    lines = [line[:, g * SEL : (g + 1) * SEL] for g in range(groups_here)]
    local = span_latents.T
    planes = [[along_plane(part, False, step) for step in (1, 3)] for part in lines]
    states = [attend_first(queries, part, local, g) for g, part in enumerate(lines)]
    after = [state for _, state in states]
    for plane in planes:
        low, high = halves(*plane, after)
        plane += [along_plane(low, False, 1), along_plane(high, False, 3)]
    outputs = [
        attend_rest(queries, *states[g], planes[g], w_uv, g) for g in range(groups_here)
    ]

    def add(*parts):
        total = functools.reduce(jnp.add, [part.astype(jnp.float32) for part in parts])
        return total.astype(jnp.bfloat16)

    blocks = list(range(RING * RING))
    far_low, far_high = project(order, outputs, w_out, blocks[2 * RING : 3 * RING], 2, [])
    by_up = along_plane(far_low, True, 1)
    by_down = along_plane(far_high, True, 3)
    own_low, own_high, up_low, up_high, down_low, down_high = project(
        order, outputs, w_out, blocks[: 2 * RING] + blocks[3 * RING :], 6, [far_low, far_high]
    )
    high_from_up = along_plane(up_high, True, 1)
    low_from_down = along_plane(down_low, True, 3)
    low_from_up = along_plane(add(up_low, by_up), True, 1)
    high_from_down = along_plane(add(down_high, by_down), True, 3)
    low = add(own_low, low_from_up, low_from_down)
    high = add(own_high, high_from_up, high_from_down)

    own_rows = token_count // (RING * RING)
    parts = [low[:own_rows], low[own_rows:], high[:own_rows], high[own_rows:]]
    return add(parts[0], *[along_plane(parts[step], False, step) for step in (1, 3, 2)])


def solution(mesh):
    return jax.shard_map(
        body,
        mesh=mesh,
        in_specs=(
            P("seq", "mp", None),
            P("seq", None),
            P("seq", "mp"),
            P(),
            P("mp", None, None),
            P("mp", None),
        ),
        out_specs=P(("seq", "mp"), None),
        check_vma=False,
    )
```

```python
import functools
import math

import jax
import jax.numpy as jnp
import numpy as np
from jax import lax
from jax.experimental import pallas as pl
from jax.experimental.pallas import tpu as pltpu
from jax.sharding import PartitionSpec as P

KV_RANK = 512
ROPE = 64
VDIM = 128
QK_HEAD = 192
BLOCK = 64
SEL = 32
QG = 128
RING = 4
ROWS = 4
LAT = KV_RANK + ROPE
KEY_WIDTH = KV_RANK + 2 * ROPE
EXP2_SCALE = float(QK_HEAD) ** (-0.5) * math.log2(math.e)
FIRST_STEP = 2
REST_STEP = 4
MARK = 16
MARK_LANES = 128
OUT_TILE = 512
FIRST_LIMIT = 10
REST_LIMIT = 14


def index_of(y, core, z, x):
    return ((y * 2 + core) * RING + z) * RING + x


def pairs(move):
    out = []
    for y in range(RING):
        for core in range(2):
            for z in range(RING):
                for x in range(RING):
                    out.append((index_of(y, core, z, x), index_of(*move(y, core, z, x))))
    return out


def send(value, move):
    return lax.ppermute(value, ("seq", "mp"), pairs(move))


def along_core(value):
    return send(value, lambda y, core, z, x: (y, 1 - core, z, x))


def along_y(value, step):
    return send(value, lambda y, core, z, x: ((y + step) % RING, core, z, x))


def along_plane(value, first, step):
    def move(y, core, z, x):
        if (core == 0) == first:
            return y, core, z, (x + step) % RING
        return y, core, (z + step) % RING, x

    return send(value, move)


CONTRACT = (((1,), (1,)), ((), ()))

def load_keys(pieces, keys):
    for row in range(ROWS):
        rope = ROWS * KV_RANK + (row // 2) * 2 * ROPE
        base = row // 2 * (keys.shape[1] // 2)
        for piece in pieces:
            for shard in range(piece.shape[0]):
                at = pl.ds(base, SEL)
                keys[row % 2, at, :KV_RANK] = piece[shard, :, row * KV_RANK : (row + 1) * KV_RANK]
                keys[row % 2, at, KV_RANK:] = piece[shard, :, rope : rope + 2 * ROPE]
                base += SEL


def load_own(local, own_keys, mine):
    own_keys[:, :LAT] = local[:, mine].T
    own_keys[:, LAT:] = jnp.zeros((QG, ROPE), own_keys.dtype)


def load_queries(queries, even, odd, mine):
    zeros = jnp.zeros((QG, ROPE), even.dtype)
    for head in range(even.shape[0] // QG):
        at = slice(head * QG, (head + 1) * QG)
        latent = queries[mine, head * LAT : head * LAT + KV_RANK]
        rope = queries[mine, head * LAT + KV_RANK : (head + 1) * LAT]
        even[at, :KV_RANK] = latent
        odd[at, :KV_RANK] = latent
        even[at, KV_RANK:] = jnp.concatenate([rope, zeros], axis=1)
        odd[at, KV_RANK:] = jnp.concatenate([zeros, rope], axis=1)


def dot_keys(a, b):
    return lax.dot_general(a, b, CONTRACT, preferred_element_type=jnp.float32)


def inside(queries, own_keys):
    scores = dot_keys(queries, own_keys[...])
    token = lax.broadcasted_iota(jnp.int32, scores.shape, 0) % QG
    slot = lax.broadcasted_iota(jnp.int32, scores.shape, 1)
    return jnp.where(slot <= token, scores, -jnp.inf)


def highest(values):
    return functools.reduce(jnp.maximum, [jnp.max(v, axis=1, keepdims=True) for v in values])


def weigh(scores, high):
    return [jnp.exp2((s - high) * EXP2_SCALE) for s in scores]


def count(weights):
    return functools.reduce(jnp.add, [jnp.sum(w, axis=1, keepdims=True) for w in weights])


def mix(weights, values):
    return jnp.dot(
        jnp.concatenate([w.astype(jnp.bfloat16) for w in weights], axis=1),
        jnp.concatenate(values, axis=0),
        preferred_element_type=jnp.float32,
    )


def raise_values(latent, w_uv, out, first):
    for head in range(latent.shape[0] // QG):
        out[:, (first + head) * VDIM : (first + head + 1) * VDIM] = jnp.dot(
            latent[head * QG : (head + 1) * QG],
            w_uv[first + head],
            preferred_element_type=jnp.float32,
        ).astype(out.dtype)


def first_kernel(group, queries, own, local, mixed, state, even, odd, keys, own_keys):
    mine = slice(group * QG, (group + 1) * QG)
    load_keys([own], keys)
    load_own(local, own_keys, mine)
    load_queries(queries, even, odd, mine)

    def scores_of(at):
        return [
            dot_keys(even[at, :], keys[0]),
            dot_keys(odd[at, :], keys[1]),
            inside(even[at, :], own_keys),
        ]

    rows = FIRST_STEP * QG
    steps = [slice(first, first + rows) for first in range(0, even.shape[0], rows)]
    ahead = scores_of(steps[0])
    for step, at in enumerate(steps):
        scores = ahead
        if step + 1 < len(steps):
            ahead = scores_of(steps[step + 1])
        high = highest(scores)
        weights = weigh(scores, high)
        values = [keys[0, :, :KV_RANK], keys[1, :, :KV_RANK], own_keys[:, :KV_RANK]]
        state[at, 0:1] = high
        state[at, 1:2] = count(weights)
        mixed[at, :] = mix(weights, values)


def rest_kernel(mixed, state, even, odd, *refs):
    *pieces, w_uv, out, keys = refs
    load_keys(pieces, keys)

    def scores_of(at):
        return [dot_keys(even[at, :], keys[0]), dot_keys(odd[at, :], keys[1])]

    rows = REST_STEP * QG
    steps = [slice(first, first + rows) for first in range(0, even.shape[0], rows)]
    ahead = scores_of(steps[0])
    for step, at in enumerate(steps):
        scores = ahead
        if step + 1 < len(steps):
            ahead = scores_of(steps[step + 1])
        before = state[at, 0:1]
        high = jnp.maximum(before, highest(scores))
        weights = weigh(scores, high)
        kept = jnp.exp2((before - high) * EXP2_SCALE)
        total = kept * state[at, 1:2] + count(weights)
        sums = mix(weights, [keys[0, :, :KV_RANK], keys[1, :, :KV_RANK]])
        latent = ((kept * mixed[at, :] + sums) / total).astype(jnp.bfloat16)
        raise_values(latent, w_uv, out, step * REST_STEP)


def vmem(number):
    return [pl.BlockSpec(memory_space=pltpu.VMEM)] * number


def attend_call(kernel, name, operands, out_shape, rows, prior, own, limit):
    keys = prior + own
    scratch = [pltpu.VMEM((2, prior // 2, KEY_WIDTH), jnp.bfloat16)]
    scratch += [pltpu.VMEM((own, KEY_WIDTH), jnp.bfloat16)] * (own > 0)
    return pl.pallas_call(
        kernel,
        in_specs=vmem(len(operands)),
        out_specs=vmem(len(out_shape)),
        out_shape=out_shape,
        scratch_shapes=scratch,
        compiler_params=pltpu.CompilerParams(vmem_limit_bytes=limit * 1024 * 1024),
        cost_estimate=pl.CostEstimate(
            flops=2 * rows * keys * (KEY_WIDTH + KV_RANK),
            bytes_accessed=2 * (rows + keys) * KEY_WIDTH,
            transcendentals=rows * keys,
        ),
        name=name,
    )(*operands)


def attend_first(queries, own, local, group):
    rows = queries.shape[1] // LAT * QG
    padded = jax.ShapeDtypeStruct((rows, KEY_WIDTH), jnp.bfloat16)
    return attend_call(
        functools.partial(first_kernel, group),
        "attend_first",
        (queries, own, local),
        [
            jax.ShapeDtypeStruct((rows, KV_RANK), jnp.float32),
            jax.ShapeDtypeStruct((rows, 2), jnp.float32),
            padded,
            padded,
        ],
        rows,
        own.shape[0] * SEL * ROWS,
        QG,
        FIRST_LIMIT,
    )


def attend_rest(state, pieces, w_uv):
    heads = w_uv.shape[0]
    return attend_call(
        rest_kernel,
        "attend_rest",
        (*state, *pieces, w_uv),
        [jax.ShapeDtypeStruct((QG, heads * VDIM), jnp.bfloat16)],
        heads * QG,
        sum(piece.shape[0] for piece in pieces) * SEL * ROWS,
        0,
        REST_LIMIT,
    )[0]


def join_kernel(a, b, out):
    out[...] = (a[...].astype(jnp.float32) + b[...].astype(jnp.float32)).astype(out.dtype)


def join(a, b):
    return pl.pallas_call(
        join_kernel,
        in_specs=vmem(2),
        out_specs=pl.BlockSpec(memory_space=pltpu.VMEM),
        out_shape=jax.ShapeDtypeStruct(a.shape, a.dtype),
        compiler_params=pltpu.CompilerParams(vmem_limit_bytes=1024 * 1024),
        cost_estimate=pl.CostEstimate(flops=0, bytes_accessed=0, transcendentals=0),
        name="join",
    )(a, b)


def halves_kernel(up, down, *refs):
    *_, low, high = refs
    half = up.shape[0] // 2
    low[...] = up[:half]
    high[...] = down[half:]


def halves(up, down, after):
    shape = jax.ShapeDtypeStruct((up.shape[0] // 2,) + up.shape[1:], up.dtype)
    return pl.pallas_call(
        halves_kernel,
        in_specs=vmem(2) + [pl.BlockSpec(memory_space=pl.ANY)] * len(after),
        out_specs=vmem(2),
        out_shape=[shape] * 2,
        compiler_params=pltpu.CompilerParams(vmem_limit_bytes=1024 * 1024),
        cost_estimate=pl.CostEstimate(flops=0, bytes_accessed=0, transcendentals=0),
        name="halves",
    )(up, down, *after)


def project_kernel(groups, blocks, tokens, order, *refs):
    heads, w_out = refs[:groups], refs[groups]
    chunks, (given, near) = refs[groups + 1 + tokens : -2], refs[-2:]
    for g, part in enumerate(heads):
        given[g * QG : (g + 1) * QG, :] = part[...]
    own_rows = given.shape[0] // (RING * RING)
    for at, block in enumerate(blocks):
        start = pl.ds(pl.multiple_of(order[block] * own_rows, own_rows), own_rows)
        near[at * own_rows : (at + 1) * own_rows, :] = given[start, :]
    rows = chunks[0].shape[0]
    for first in range(0, w_out.shape[1], OUT_TILE):
        at = slice(first, first + OUT_TILE)
        terms = jnp.dot(near[...], w_out[:, at], preferred_element_type=jnp.float32)
        for step, chunk in enumerate(chunks):
            chunk[:, at] = terms[step * rows : (step + 1) * rows].astype(chunk.dtype)


def project(order, heads, w_out, blocks, pieces, after):
    groups = len(heads)
    depth, columns = w_out.shape
    rows = len(blocks) * (groups * QG // (RING * RING))
    return pl.pallas_call(
        functools.partial(project_kernel, groups, blocks, len(after)),
        in_specs=[pl.BlockSpec(memory_space=pltpu.SMEM)]
        + vmem(groups + 1)
        + [pl.BlockSpec(memory_space=pl.ANY)] * len(after),
        out_specs=vmem(pieces),
        out_shape=[jax.ShapeDtypeStruct((rows // pieces, columns), jnp.bfloat16)] * pieces,
        scratch_shapes=[
            pltpu.VMEM((groups * QG, depth), jnp.bfloat16),
            pltpu.VMEM((rows, depth), jnp.bfloat16),
        ],
        compiler_params=pltpu.CompilerParams(vmem_limit_bytes=6 * 1024 * 1024),
        cost_estimate=pl.CostEstimate(
            flops=2 * rows * depth * columns,
            bytes_accessed=2 * depth * columns,
            transcendentals=0,
        ),
        name="project",
    )(order, *heads, w_out, *after)


def block_orders():
    orders = np.zeros((2, RING, RING, RING, RING), np.int32)
    for core, z, x, one, two in np.ndindex(*orders.shape):
        if core == 0:
            orders[core, z, x, one, two] = (z + two) % RING * RING + (x + one) % RING
        else:
            orders[core, z, x, one, two] = (z + one) % RING * RING + (x + two) % RING
    return orders.reshape(2 * RING * RING, RING * RING)


def body(cache, span_latents, queries, selected, w_uv, w_out):
    seq_index = lax.axis_index("seq")
    mp_index = lax.axis_index("mp")
    y_index, core = seq_index // 2, seq_index % 2
    blocks_here, block_rows, latent_width = cache.shape
    token_count = queries.shape[0]
    groups_here = token_count // QG
    slots = groups_here * SEL

    order = lax.dynamic_index_in_dim(
        jnp.asarray(block_orders()), core * RING * RING + mp_index, 0, keepdims=False
    )
    selected, order = lax.optimization_barrier((selected, order))
    requests = selected.reshape(RING, 2, slots) - seq_index * blocks_here
    requests = jnp.roll(requests, -y_index, axis=0)
    requests = jnp.where(core == 0, requests, requests[:, ::-1])
    flat = jnp.concatenate(
        [
            cache[:, :, :KV_RANK].reshape(blocks_here, block_rows * KV_RANK),
            cache[:, :, KV_RANK:].reshape(blocks_here, block_rows * ROPE),
        ],
        axis=1,
    )

    picks = requests.transpose(1, 0, 2).reshape(-1)
    onehot = (picks[:, None] == lax.broadcasted_iota(jnp.int32, (1, blocks_here), 1)).astype(
        cache.dtype
    )
    rows = jnp.dot(onehot, flat, preferred_element_type=jnp.float32).astype(cache.dtype)
    rows = rows.reshape(2, RING, slots, block_rows * latent_width)
    both = rows[0] + along_core(rows[1])

    half = slots // 2
    own, up, far, down = both
    by_up = along_y(far[:half], 1)
    by_down = along_y(far[half:], 3)
    high_from_up = along_y(up[half:], 1)
    low_from_down = along_y(down[:half], 3)
    low_from_up = along_y(join(up[:half], by_up), 1)
    high_from_down = along_y(join(down[half:], by_down), 3)
    low = own[:half] + low_from_up + low_from_down
    high = own[half:] + high_from_up + high_from_down
    shard = jnp.concatenate([low, high], axis=0)

    line = jnp.stack([shard] + [along_plane(shard, True, step) for step in (1, 3, 2)])
    lines = [line[:, g * SEL : (g + 1) * SEL] for g in range(groups_here)]
    local = span_latents.T
    planes = [[along_plane(part, False, step) for step in (1, 3)] for part in lines]
    states = [attend_first(queries, part, local, g) for g, part in enumerate(lines)]
    after = [state[1] for state in states]
    for plane in planes:
        low, high = halves(*plane, after)
        plane += [along_plane(low, False, 1), along_plane(high, False, 3)]
    outputs = [
        attend_rest(states[g], planes[g], w_uv) for g in range(groups_here)
    ]

    def add(*parts):
        total = functools.reduce(jnp.add, [part.astype(jnp.float32) for part in parts])
        return total.astype(jnp.bfloat16)

    blocks = list(range(RING * RING))
    ready = along_core(outputs[-1][:MARK, :MARK_LANES])
    far_low, far_high = project(order, outputs, w_out, blocks[2 * RING : 3 * RING], 2, [ready])
    by_up = along_plane(far_low, True, 1)
    by_down = along_plane(far_high, True, 3)
    own_low, own_high, up_low, up_high, down_low, down_high = project(
        order, outputs, w_out, blocks[: 2 * RING] + blocks[3 * RING :], 6, [far_low, far_high]
    )
    high_from_up = along_plane(up_high, True, 1)
    low_from_down = along_plane(down_low, True, 3)
    low_from_up = along_plane(add(up_low, by_up), True, 1)
    high_from_down = along_plane(add(down_high, by_down), True, 3)
    low = add(own_low, low_from_up, low_from_down)
    high = add(own_high, high_from_up, high_from_down)

    own_rows = token_count // (RING * RING)
    parts = [low[:own_rows], low[own_rows:], high[:own_rows], high[own_rows:]]
    return add(parts[0], *[along_plane(parts[step], False, step) for step in (1, 3, 2)])


def solution(mesh):
    return jax.shard_map(
        body,
        mesh=mesh,
        in_specs=(
            P("seq", "mp", None),
            P("seq", None),
            P("seq", "mp"),
            P(),
            P("mp", None, None),
            P("mp", None),
        ),
        out_specs=P(("seq", "mp"), None),
        check_vma=False,
    )
```

```python
import functools
import math

import jax
import jax.numpy as jnp
import numpy as np
from jax import lax
from jax.experimental import pallas as pl
from jax.experimental.pallas import tpu as pltpu
from jax.sharding import PartitionSpec as P

KV_RANK = 512
ROPE = 64
VDIM = 128
QK_HEAD = 192
BLOCK = 64
SEL = 32
QG = 128
RING = 4
ROWS = 4
LAT = KV_RANK + ROPE
KEY_WIDTH = KV_RANK + 2 * ROPE
EXP2_SCALE = float(QK_HEAD) ** (-0.5) * math.log2(math.e)
FIRST_STEP = 2
REST_STEP = 4
MARK = 16
MARK_LANES = 128
OUT_TILE = 512
FIRST_LIMIT = 10
REST_LIMIT = 14


def index_of(y, core, z, x):
    return ((y * 2 + core) * RING + z) * RING + x


def pairs(move):
    out = []
    for y in range(RING):
        for core in range(2):
            for z in range(RING):
                for x in range(RING):
                    out.append((index_of(y, core, z, x), index_of(*move(y, core, z, x))))
    return out


def send(value, move):
    return lax.ppermute(value, ("seq", "mp"), pairs(move))


def along_core(value):
    return send(value, lambda y, core, z, x: (y, 1 - core, z, x))


def along_y(value, step):
    return send(value, lambda y, core, z, x: ((y + step) % RING, core, z, x))


def along_plane(value, first, step):
    def move(y, core, z, x):
        if (core == 0) == first:
            return y, core, z, (x + step) % RING
        return y, core, (z + step) % RING, x

    return send(value, move)


CONTRACT = (((1,), (1,)), ((), ()))

def load_keys(pieces, keys):
    for row in range(ROWS):
        rope = ROWS * KV_RANK + (row // 2) * 2 * ROPE
        base = row // 2 * (keys.shape[1] // 2)
        for piece in pieces:
            for shard in range(piece.shape[0]):
                at = pl.ds(base, SEL)
                keys[row % 2, at, :KV_RANK] = piece[shard, :, row * KV_RANK : (row + 1) * KV_RANK]
                keys[row % 2, at, KV_RANK:] = piece[shard, :, rope : rope + 2 * ROPE]
                base += SEL


def load_own(local, own_keys, mine):
    own_keys[:, :LAT] = local[:, mine].T
    own_keys[:, LAT:] = jnp.zeros((QG, ROPE), own_keys.dtype)


def load_queries(queries, even, odd, mine):
    zeros = jnp.zeros((QG, ROPE), even.dtype)
    for head in range(even.shape[0] // QG):
        at = slice(head * QG, (head + 1) * QG)
        latent = queries[mine, head * LAT : head * LAT + KV_RANK]
        rope = queries[mine, head * LAT + KV_RANK : (head + 1) * LAT]
        even[at, :KV_RANK] = latent
        odd[at, :KV_RANK] = latent
        even[at, KV_RANK:] = jnp.concatenate([rope, zeros], axis=1)
        odd[at, KV_RANK:] = jnp.concatenate([zeros, rope], axis=1)


def dot_keys(a, b):
    return lax.dot_general(a, b, CONTRACT, preferred_element_type=jnp.float32)


def inside(queries, own_keys):
    scores = dot_keys(queries, own_keys[...])
    token = lax.broadcasted_iota(jnp.int32, scores.shape, 0) % QG
    slot = lax.broadcasted_iota(jnp.int32, scores.shape, 1)
    return jnp.where(slot <= token, scores, -jnp.inf)


def highest(values):
    return functools.reduce(jnp.maximum, [jnp.max(v, axis=1, keepdims=True) for v in values])


def weigh(scores, high):
    return [jnp.exp2((s - high) * EXP2_SCALE) for s in scores]


def count(weights):
    return functools.reduce(jnp.add, [jnp.sum(w, axis=1, keepdims=True) for w in weights])


def mix(weights, values):
    return jnp.dot(
        jnp.concatenate([w.astype(jnp.bfloat16) for w in weights], axis=1),
        jnp.concatenate(values, axis=0),
        preferred_element_type=jnp.float32,
    )


def first_kernel(group, queries, own, local, mixed, state, even, odd, keys, own_keys):
    mine = slice(group * QG, (group + 1) * QG)
    load_keys([own], keys)
    load_own(local, own_keys, mine)
    load_queries(queries, even, odd, mine)

    def scores_of(at):
        return [
            dot_keys(even[at, :], keys[0]),
            dot_keys(odd[at, :], keys[1]),
            inside(even[at, :], own_keys),
        ]

    rows = FIRST_STEP * QG
    steps = [slice(first, first + rows) for first in range(0, even.shape[0], rows)]
    ahead = scores_of(steps[0])
    for step, at in enumerate(steps):
        scores = ahead
        if step + 1 < len(steps):
            ahead = scores_of(steps[step + 1])
        high = highest(scores)
        weights = weigh(scores, high)
        values = [keys[0, :, :KV_RANK], keys[1, :, :KV_RANK], own_keys[:, :KV_RANK]]
        state[at, 0:1] = high
        state[at, 1:2] = count(weights)
        mixed[at, :] = mix(weights, values)


def rest_kernel(mixed, state, even, odd, *refs):
    *pieces, out, keys = refs
    load_keys(pieces, keys)

    def scores_of(at):
        return [dot_keys(even[at, :], keys[0]), dot_keys(odd[at, :], keys[1])]

    rows = REST_STEP * QG
    steps = [slice(first, first + rows) for first in range(0, even.shape[0], rows)]
    ahead = scores_of(steps[0])
    for step, at in enumerate(steps):
        scores = ahead
        if step + 1 < len(steps):
            ahead = scores_of(steps[step + 1])
        before = state[at, 0:1]
        high = jnp.maximum(before, highest(scores))
        weights = weigh(scores, high)
        kept = jnp.exp2((before - high) * EXP2_SCALE)
        total = kept * state[at, 1:2] + count(weights)
        sums = mix(weights, [keys[0, :, :KV_RANK], keys[1, :, :KV_RANK]])
        out[at, :] = ((kept * mixed[at, :] + sums) / total).astype(out.dtype)


def vmem(number):
    return [pl.BlockSpec(memory_space=pltpu.VMEM)] * number


def attend_call(kernel, name, operands, out_shape, rows, prior, own, limit):
    keys = prior + own
    scratch = [pltpu.VMEM((2, prior // 2, KEY_WIDTH), jnp.bfloat16)]
    scratch += [pltpu.VMEM((own, KEY_WIDTH), jnp.bfloat16)] * (own > 0)
    return pl.pallas_call(
        kernel,
        in_specs=vmem(len(operands)),
        out_specs=vmem(len(out_shape)),
        out_shape=out_shape,
        scratch_shapes=scratch,
        compiler_params=pltpu.CompilerParams(vmem_limit_bytes=limit * 1024 * 1024),
        cost_estimate=pl.CostEstimate(
            flops=2 * rows * keys * (KEY_WIDTH + KV_RANK),
            bytes_accessed=2 * (rows + keys) * KEY_WIDTH,
            transcendentals=rows * keys,
        ),
        name=name,
    )(*operands)


def attend_first(queries, own, local, group):
    rows = queries.shape[1] // LAT * QG
    padded = jax.ShapeDtypeStruct((rows, KEY_WIDTH), jnp.bfloat16)
    return attend_call(
        functools.partial(first_kernel, group),
        "attend_first",
        (queries, own, local),
        [
            jax.ShapeDtypeStruct((rows, KV_RANK), jnp.float32),
            jax.ShapeDtypeStruct((rows, 2), jnp.float32),
            padded,
            padded,
        ],
        rows,
        own.shape[0] * SEL * ROWS,
        QG,
        FIRST_LIMIT,
    )


def attend_rest(state, pieces):
    rows = state[0].shape[0]
    return attend_call(
        rest_kernel,
        "attend_rest",
        (*state, *pieces),
        [jax.ShapeDtypeStruct((rows, KV_RANK), jnp.bfloat16)],
        rows,
        sum(piece.shape[0] for piece in pieces) * SEL * ROWS,
        0,
        REST_LIMIT,
    )[0]


def join_kernel(a, b, out):
    out[...] = (a[...].astype(jnp.float32) + b[...].astype(jnp.float32)).astype(out.dtype)


def join(a, b):
    return pl.pallas_call(
        join_kernel,
        in_specs=vmem(2),
        out_specs=pl.BlockSpec(memory_space=pltpu.VMEM),
        out_shape=jax.ShapeDtypeStruct(a.shape, a.dtype),
        compiler_params=pltpu.CompilerParams(vmem_limit_bytes=1024 * 1024),
        cost_estimate=pl.CostEstimate(flops=0, bytes_accessed=0, transcendentals=0),
        name="join",
    )(a, b)


def stack_kernel(*refs):
    shards, lines = refs[:RING], refs[RING + 1 :]
    for g, line in enumerate(lines):
        for at, shard in enumerate(shards):
            line[at] = shard[g * SEL : (g + 1) * SEL, :]


def stack_lines(shards, after):
    slots, width = shards[0].shape
    shape = jax.ShapeDtypeStruct((RING, SEL, width), shards[0].dtype)
    return pl.pallas_call(
        stack_kernel,
        in_specs=vmem(RING) + [pl.BlockSpec(memory_space=pl.ANY)],
        out_specs=vmem(slots // SEL),
        out_shape=[shape] * (slots // SEL),
        compiler_params=pltpu.CompilerParams(vmem_limit_bytes=1024 * 1024),
        cost_estimate=pl.CostEstimate(flops=0, bytes_accessed=0, transcendentals=0),
        name="stack",
    )(*shards, after)


def halves_kernel(up, down, *refs):
    *_, low, high = refs
    half = up.shape[0] // 2
    low[...] = up[:half]
    high[...] = down[half:]


def halves(up, down, after):
    shape = jax.ShapeDtypeStruct((up.shape[0] // 2,) + up.shape[1:], up.dtype)
    return pl.pallas_call(
        halves_kernel,
        in_specs=vmem(2) + [pl.BlockSpec(memory_space=pl.ANY)] * len(after),
        out_specs=vmem(2),
        out_shape=[shape] * 2,
        compiler_params=pltpu.CompilerParams(vmem_limit_bytes=1024 * 1024),
        cost_estimate=pl.CostEstimate(flops=0, bytes_accessed=0, transcendentals=0),
        name="halves",
    )(up, down, *after)


def terms(rows, w_out, chunks):
    count = chunks[0].shape[0]
    for first in range(0, w_out.shape[1], OUT_TILE):
        at = slice(first, first + OUT_TILE)
        total = jnp.dot(rows, w_out[:, at], preferred_element_type=jnp.float32)
        for step, chunk in enumerate(chunks):
            chunk[:, at] = total[step * count : (step + 1) * count].astype(chunk.dtype)


def project_far_kernel(groups, order, *refs):
    latents, (w_uv, w_out, _, near, low, high, values, far) = refs[:groups], refs[groups:]
    for head in range(w_uv.shape[0]):
        mine = [part[head * QG : (head + 1) * QG, :] for part in latents]
        values[:, head * VDIM : (head + 1) * VDIM] = jnp.dot(
            jnp.concatenate(mine, axis=0), w_uv[head], preferred_element_type=jnp.float32
        ).astype(values.dtype)
    own_rows = values.shape[0] // (RING * RING)
    for block in range(RING * RING):
        start = pl.ds(pl.multiple_of(order[block] * own_rows, own_rows), own_rows)
        distance, place = divmod(block, RING)
        if distance == 2:
            far[place * own_rows : (place + 1) * own_rows, :] = values[start, :]
        else:
            at = (min(distance, 2) * RING + place) * own_rows
            near[at : at + own_rows, :] = values[start, :]
    terms(far[...], w_out, (low, high))


def project_far(order, latents, w_uv, w_out, after):
    groups = len(latents)
    depth, columns = w_out.shape
    rows = groups * QG
    share = rows // RING
    piece = jax.ShapeDtypeStruct((share // 2, columns), jnp.bfloat16)
    return pl.pallas_call(
        functools.partial(project_far_kernel, groups),
        in_specs=[pl.BlockSpec(memory_space=pltpu.SMEM)]
        + vmem(groups + 2)
        + [pl.BlockSpec(memory_space=pl.ANY)],
        out_specs=vmem(3),
        out_shape=[jax.ShapeDtypeStruct((rows - share, depth), jnp.bfloat16), piece, piece],
        scratch_shapes=[
            pltpu.VMEM((rows, depth), jnp.bfloat16),
            pltpu.VMEM((share, depth), jnp.bfloat16),
        ],
        compiler_params=pltpu.CompilerParams(vmem_limit_bytes=6 * 1024 * 1024),
        cost_estimate=pl.CostEstimate(
            flops=2 * share * depth * columns,
            bytes_accessed=2 * depth * columns,
            transcendentals=0,
        ),
        name="project_far",
    )(order, *latents, w_uv, w_out, after)


def project_near_kernel(near, w_out, *refs):
    terms(near[...], w_out, refs[-2 * (RING - 1) :])


def project_near(near, w_out, after):
    rows, depth = near.shape
    columns = w_out.shape[1]
    pieces = 2 * (RING - 1)
    return pl.pallas_call(
        project_near_kernel,
        in_specs=vmem(2) + [pl.BlockSpec(memory_space=pl.ANY)] * len(after),
        out_specs=vmem(pieces),
        out_shape=[jax.ShapeDtypeStruct((rows // pieces, columns), jnp.bfloat16)] * pieces,
        compiler_params=pltpu.CompilerParams(vmem_limit_bytes=4 * 1024 * 1024),
        cost_estimate=pl.CostEstimate(
            flops=2 * rows * depth * columns,
            bytes_accessed=2 * depth * columns,
            transcendentals=0,
        ),
        name="project_near",
    )(near, w_out, *after)


def block_orders():
    orders = np.zeros((2, RING, RING, RING, RING), np.int32)
    for core, z, x, one, two in np.ndindex(*orders.shape):
        if core == 1:
            orders[core, z, x, one, two] = (z + two) % RING * RING + (x + one) % RING
        else:
            orders[core, z, x, one, two] = (z + one) % RING * RING + (x + two) % RING
    return orders.reshape(2 * RING * RING, RING * RING)


def body(cache, span_latents, queries, selected, w_uv, w_out):
    seq_index = lax.axis_index("seq")
    mp_index = lax.axis_index("mp")
    y_index, core = seq_index // 2, seq_index % 2
    blocks_here, block_rows, latent_width = cache.shape
    token_count = queries.shape[0]
    groups_here = token_count // QG
    slots = groups_here * SEL

    order = lax.dynamic_index_in_dim(
        jnp.asarray(block_orders()), core * RING * RING + mp_index, 0, keepdims=False
    )
    selected, order = lax.optimization_barrier((selected, order))
    requests = selected.reshape(RING, 2, slots) - seq_index * blocks_here
    requests = jnp.roll(requests, -y_index, axis=0)
    requests = jnp.where(core == 0, requests, requests[:, ::-1])
    flat = jnp.concatenate(
        [
            cache[:, :, :KV_RANK].reshape(blocks_here, block_rows * KV_RANK),
            cache[:, :, KV_RANK:].reshape(blocks_here, block_rows * ROPE),
        ],
        axis=1,
    )

    picks = requests.transpose(1, 0, 2).reshape(-1)
    onehot = (picks[:, None] == lax.broadcasted_iota(jnp.int32, (1, blocks_here), 1)).astype(
        cache.dtype
    )
    rows = jnp.dot(onehot, flat, preferred_element_type=jnp.float32).astype(cache.dtype)
    rows = rows.reshape(2, RING, slots, block_rows * latent_width)
    both = rows[0] + along_core(rows[1])

    half = slots // 2
    own, up, far, down = both
    by_up = along_y(far[:half], 1)
    by_down = along_y(far[half:], 3)
    high_from_up = along_y(up[half:], 1)
    low_from_down = along_y(down[:half], 3)
    low_from_up = along_y(join(up[:half], by_up), 1)
    high_from_down = along_y(join(down[half:], by_down), 3)
    low = own[:half] + low_from_up + low_from_down
    high = own[half:] + high_from_up + high_from_down
    shard = jnp.concatenate([low, high], axis=0)

    others = [along_plane(shard, True, step) for step in (1, 3, 2)]
    ready = along_core(others[-1][:MARK, :MARK_LANES])
    lines = stack_lines([shard] + others, ready)

    local = span_latents.T
    planes = [[along_plane(part, False, step) for step in (1, 3)] for part in lines]
    states = [attend_first(queries, part, local, g) for g, part in enumerate(lines)]
    after = [state[1] for state in states]
    for plane in planes:
        low, high = halves(*plane, after)
        plane += [along_plane(low, False, 1), along_plane(high, False, 3)]
    outputs = [
        attend_rest(states[g], planes[g]) for g in range(groups_here)
    ]

    def add(*parts):
        total = functools.reduce(jnp.add, [part.astype(jnp.float32) for part in parts])
        return total.astype(jnp.bfloat16)

    ready = along_core(outputs[-1][:MARK, :MARK_LANES])
    near, far_low, far_high = project_far(order, outputs, w_uv, w_out, ready)
    by_up = along_plane(far_low, False, 1)
    by_down = along_plane(far_high, False, 3)
    own_low, own_high, up_low, up_high, down_low, down_high = project_near(
        near, w_out, [far_low, far_high]
    )
    high_from_up = along_plane(up_high, False, 1)
    low_from_down = along_plane(down_low, False, 3)
    low_from_up = along_plane(add(up_low, by_up), False, 1)
    high_from_down = along_plane(add(down_high, by_down), False, 3)
    low = add(own_low, low_from_up, low_from_down)
    high = add(own_high, high_from_up, high_from_down)

    own_rows = token_count // (RING * RING)
    parts = [low[:own_rows], low[own_rows:], high[:own_rows], high[own_rows:]]
    return add(parts[0], *[along_plane(parts[step], True, step) for step in (1, 3, 2)])


def solution(mesh):
    return jax.shard_map(
        body,
        mesh=mesh,
        in_specs=(
            P("seq", "mp", None),
            P("seq", None),
            P("seq", "mp"),
            P(),
            P("mp", None, None),
            P("mp", None),
        ),
        out_specs=P(("seq", "mp"), None),
        check_vma=False,
    )
```

```python
import functools
import math

import jax
import jax.numpy as jnp
import numpy as np
from jax import lax
from jax.experimental import pallas as pl
from jax.experimental.pallas import tpu as pltpu
from jax.sharding import PartitionSpec as P

KV_RANK = 512
ROPE = 64
VDIM = 128
QK_HEAD = 192
BLOCK = 64
SEL = 32
QG = 128
RING = 4
ROWS = 4
LAT = KV_RANK + ROPE
KEY_WIDTH = KV_RANK + 2 * ROPE
EXP2_SCALE = float(QK_HEAD) ** (-0.5) * math.log2(math.e)
FIRST_STEP = 2
REST_STEP = 4
MARK = 16
MARK_LANES = 128
OUT_TILE = 1024
FIRST_LIMIT = 10
REST_LIMIT = 14


def index_of(y, core, z, x):
    return ((y * 2 + core) * RING + z) * RING + x


def pairs(move):
    out = []
    for y in range(RING):
        for core in range(2):
            for z in range(RING):
                for x in range(RING):
                    out.append((index_of(y, core, z, x), index_of(*move(y, core, z, x))))
    return out


def send(value, move):
    return lax.ppermute(value, ("seq", "mp"), pairs(move))


def along_core(value):
    return send(value, lambda y, core, z, x: (y, 1 - core, z, x))


def along_y(value, step):
    return send(value, lambda y, core, z, x: ((y + step) % RING, core, z, x))


def along_plane(value, first, step):
    def move(y, core, z, x):
        if (core == 0) == first:
            return y, core, z, (x + step) % RING
        return y, core, (z + step) % RING, x

    return send(value, move)


CONTRACT = (((1,), (1,)), ((), ()))

def load_keys(pieces, keys):
    for row in range(ROWS):
        rope = ROWS * KV_RANK + (row // 2) * 2 * ROPE
        base = row // 2 * (keys.shape[1] // 2)
        for piece in pieces:
            for shard in range(piece.shape[0]):
                at = pl.ds(base, SEL)
                keys[row % 2, at, :KV_RANK] = piece[shard, :, row * KV_RANK : (row + 1) * KV_RANK]
                keys[row % 2, at, KV_RANK:] = piece[shard, :, rope : rope + 2 * ROPE]
                base += SEL


def load_own(local, own_keys, mine):
    own_keys[:, :LAT] = local[:, mine].T
    own_keys[:, LAT:] = jnp.zeros((QG, ROPE), own_keys.dtype)


def load_queries(queries, even, odd, mine):
    zeros = jnp.zeros((QG, ROPE), even.dtype)
    for head in range(even.shape[0] // QG):
        at = slice(head * QG, (head + 1) * QG)
        latent = queries[mine, head * LAT : head * LAT + KV_RANK]
        rope = queries[mine, head * LAT + KV_RANK : (head + 1) * LAT]
        even[at, :KV_RANK] = latent
        odd[at, :KV_RANK] = latent
        even[at, KV_RANK:] = jnp.concatenate([rope, zeros], axis=1)
        odd[at, KV_RANK:] = jnp.concatenate([zeros, rope], axis=1)


def dot_keys(a, b):
    return lax.dot_general(a, b, CONTRACT, preferred_element_type=jnp.float32)


def inside(queries, own_keys):
    scores = dot_keys(queries, own_keys[...])
    token = lax.broadcasted_iota(jnp.int32, scores.shape, 0) % QG
    slot = lax.broadcasted_iota(jnp.int32, scores.shape, 1)
    return jnp.where(slot <= token, scores, -jnp.inf)


def highest(values):
    return functools.reduce(jnp.maximum, [jnp.max(v, axis=1, keepdims=True) for v in values])


def weigh(scores, high):
    return [jnp.exp2((s - high) * EXP2_SCALE) for s in scores]


def count(weights):
    return functools.reduce(jnp.add, [jnp.sum(w, axis=1, keepdims=True) for w in weights])


def mix(weights, values):
    return jnp.dot(
        jnp.concatenate([w.astype(jnp.bfloat16) for w in weights], axis=1),
        jnp.concatenate(values, axis=0),
        preferred_element_type=jnp.float32,
    )


def first_kernel(group, queries, own, local, mixed, state, even, odd, keys, own_keys):
    mine = slice(group * QG, (group + 1) * QG)
    load_keys([own], keys)
    load_own(local, own_keys, mine)
    load_queries(queries, even, odd, mine)

    def scores_of(at):
        return [
            dot_keys(even[at, :], keys[0]),
            dot_keys(odd[at, :], keys[1]),
            inside(even[at, :], own_keys),
        ]

    rows = FIRST_STEP * QG
    steps = [slice(first, first + rows) for first in range(0, even.shape[0], rows)]
    ahead = scores_of(steps[0])
    for step, at in enumerate(steps):
        scores = ahead
        if step + 1 < len(steps):
            ahead = scores_of(steps[step + 1])
        high = highest(scores)
        weights = weigh(scores, high)
        values = [keys[0, :, :KV_RANK], keys[1, :, :KV_RANK], own_keys[:, :KV_RANK]]
        state[at, 0:1] = high
        state[at, 1:2] = count(weights)
        mixed[at, :] = mix(weights, values)


def rest_kernel(mixed, state, even, odd, *refs):
    *pieces, out, keys = refs
    load_keys(pieces, keys)

    def scores_of(at):
        return [dot_keys(even[at, :], keys[0]), dot_keys(odd[at, :], keys[1])]

    rows = REST_STEP * QG
    steps = [slice(first, first + rows) for first in range(0, even.shape[0], rows)]
    ahead = scores_of(steps[0])
    for step, at in enumerate(steps):
        scores = ahead
        if step + 1 < len(steps):
            ahead = scores_of(steps[step + 1])
        before = state[at, 0:1]
        high = jnp.maximum(before, highest(scores))
        weights = weigh(scores, high)
        kept = jnp.exp2((before - high) * EXP2_SCALE)
        total = kept * state[at, 1:2] + count(weights)
        sums = mix(weights, [keys[0, :, :KV_RANK], keys[1, :, :KV_RANK]])
        out[at, :] = ((kept * mixed[at, :] + sums) / total).astype(out.dtype)


def vmem(number):
    return [pl.BlockSpec(memory_space=pltpu.VMEM)] * number


def attend_call(kernel, name, operands, out_shape, rows, prior, own, limit):
    keys = prior + own
    scratch = [pltpu.VMEM((2, prior // 2, KEY_WIDTH), jnp.bfloat16)]
    scratch += [pltpu.VMEM((own, KEY_WIDTH), jnp.bfloat16)] * (own > 0)
    return pl.pallas_call(
        kernel,
        in_specs=vmem(len(operands)),
        out_specs=vmem(len(out_shape)),
        out_shape=out_shape,
        scratch_shapes=scratch,
        compiler_params=pltpu.CompilerParams(vmem_limit_bytes=limit * 1024 * 1024),
        cost_estimate=pl.CostEstimate(
            flops=2 * rows * keys * (KEY_WIDTH + KV_RANK),
            bytes_accessed=2 * (rows + keys) * KEY_WIDTH,
            transcendentals=rows * keys,
        ),
        name=name,
    )(*operands)


def attend_first(queries, own, local, group):
    rows = queries.shape[1] // LAT * QG
    padded = jax.ShapeDtypeStruct((rows, KEY_WIDTH), jnp.bfloat16)
    return attend_call(
        functools.partial(first_kernel, group),
        "attend_first",
        (queries, own, local),
        [
            jax.ShapeDtypeStruct((rows, KV_RANK), jnp.float32),
            jax.ShapeDtypeStruct((rows, 2), jnp.float32),
            padded,
            padded,
        ],
        rows,
        own.shape[0] * SEL * ROWS,
        QG,
        FIRST_LIMIT,
    )


def attend_rest(state, pieces):
    rows = state[0].shape[0]
    return attend_call(
        rest_kernel,
        "attend_rest",
        (*state, *pieces),
        [jax.ShapeDtypeStruct((rows, KV_RANK), jnp.bfloat16)],
        rows,
        sum(piece.shape[0] for piece in pieces) * SEL * ROWS,
        0,
        REST_LIMIT,
    )[0]


def join_kernel(a, b, out):
    out[...] = (a[...].astype(jnp.float32) + b[...].astype(jnp.float32)).astype(out.dtype)


def join(a, b):
    return pl.pallas_call(
        join_kernel,
        in_specs=vmem(2),
        out_specs=pl.BlockSpec(memory_space=pltpu.VMEM),
        out_shape=jax.ShapeDtypeStruct(a.shape, a.dtype),
        compiler_params=pltpu.CompilerParams(vmem_limit_bytes=1024 * 1024),
        cost_estimate=pl.CostEstimate(flops=0, bytes_accessed=0, transcendentals=0),
        name="join",
    )(a, b)


def stack_kernel(*refs):
    shards, lines = refs[:RING], refs[RING + 1 :]
    for g, line in enumerate(lines):
        for at, shard in enumerate(shards):
            line[at] = shard[g * SEL : (g + 1) * SEL, :]


def stack_lines(shards, after):
    slots, width = shards[0].shape
    shape = jax.ShapeDtypeStruct((RING, SEL, width), shards[0].dtype)
    return pl.pallas_call(
        stack_kernel,
        in_specs=vmem(RING) + [pl.BlockSpec(memory_space=pl.ANY)],
        out_specs=vmem(slots // SEL),
        out_shape=[shape] * (slots // SEL),
        compiler_params=pltpu.CompilerParams(vmem_limit_bytes=1024 * 1024),
        cost_estimate=pl.CostEstimate(flops=0, bytes_accessed=0, transcendentals=0),
        name="stack",
    )(*shards, after)


def halves_kernel(up, down, *refs):
    *_, low, high = refs
    half = up.shape[0] // 2
    low[...] = up[:half]
    high[...] = down[half:]


def halves(up, down, after):
    shape = jax.ShapeDtypeStruct((up.shape[0] // 2,) + up.shape[1:], up.dtype)
    return pl.pallas_call(
        halves_kernel,
        in_specs=vmem(2) + [pl.BlockSpec(memory_space=pl.ANY)] * len(after),
        out_specs=vmem(2),
        out_shape=[shape] * 2,
        compiler_params=pltpu.CompilerParams(vmem_limit_bytes=1024 * 1024),
        cost_estimate=pl.CostEstimate(flops=0, bytes_accessed=0, transcendentals=0),
        name="halves",
    )(up, down, *after)


def terms(rows, w_out, chunks):
    count = chunks[0].shape[0]
    for first in range(0, w_out.shape[1], OUT_TILE):
        at = slice(first, first + OUT_TILE)
        total = jnp.dot(rows, w_out[:, at], preferred_element_type=jnp.float32)
        for step, chunk in enumerate(chunks):
            chunk[:, at] = total[step * count : (step + 1) * count].astype(chunk.dtype)


def project_far_kernel(groups, order, *refs):
    latents, (w_uv, w_out, _, near, low, high, values, far) = refs[:groups], refs[groups:]
    for head in range(w_uv.shape[0]):
        mine = [part[head * QG : (head + 1) * QG, :] for part in latents]
        values[:, head * VDIM : (head + 1) * VDIM] = jnp.dot(
            jnp.concatenate(mine, axis=0), w_uv[head], preferred_element_type=jnp.float32
        ).astype(values.dtype)
    own_rows = values.shape[0] // (RING * RING)
    for block in range(RING * RING):
        start = pl.ds(pl.multiple_of(order[block] * own_rows, own_rows), own_rows)
        distance, place = divmod(block, RING)
        if distance == 2:
            far[place * own_rows : (place + 1) * own_rows, :] = values[start, :]
        else:
            at = (min(distance, 2) * RING + place) * own_rows
            near[at : at + own_rows, :] = values[start, :]
    terms(far[...], w_out, (low, high))


def project_far(order, latents, w_uv, w_out, after):
    groups = len(latents)
    depth, columns = w_out.shape
    rows = groups * QG
    share = rows // RING
    piece = jax.ShapeDtypeStruct((share // 2, columns), jnp.bfloat16)
    return pl.pallas_call(
        functools.partial(project_far_kernel, groups),
        in_specs=[pl.BlockSpec(memory_space=pltpu.SMEM)]
        + vmem(groups + 2)
        + [pl.BlockSpec(memory_space=pl.ANY)],
        out_specs=vmem(3),
        out_shape=[jax.ShapeDtypeStruct((rows - share, depth), jnp.bfloat16), piece, piece],
        scratch_shapes=[
            pltpu.VMEM((rows, depth), jnp.bfloat16),
            pltpu.VMEM((share, depth), jnp.bfloat16),
        ],
        compiler_params=pltpu.CompilerParams(vmem_limit_bytes=6 * 1024 * 1024),
        cost_estimate=pl.CostEstimate(
            flops=2 * share * depth * columns,
            bytes_accessed=2 * depth * columns,
            transcendentals=0,
        ),
        name="project_far",
    )(order, *latents, w_uv, w_out, after)


def project_near_kernel(near, w_out, *refs):
    terms(near[...], w_out, refs[-2 * (RING - 1) :])


def project_near(near, w_out, after):
    rows, depth = near.shape
    columns = w_out.shape[1]
    pieces = 2 * (RING - 1)
    return pl.pallas_call(
        project_near_kernel,
        in_specs=vmem(2) + [pl.BlockSpec(memory_space=pl.ANY)] * len(after),
        out_specs=vmem(pieces),
        out_shape=[jax.ShapeDtypeStruct((rows // pieces, columns), jnp.bfloat16)] * pieces,
        compiler_params=pltpu.CompilerParams(vmem_limit_bytes=4 * 1024 * 1024),
        cost_estimate=pl.CostEstimate(
            flops=2 * rows * depth * columns,
            bytes_accessed=2 * depth * columns,
            transcendentals=0,
        ),
        name="project_near",
    )(near, w_out, *after)


def block_orders():
    orders = np.zeros((2, RING, RING, RING, RING), np.int32)
    for core, z, x, one, two in np.ndindex(*orders.shape):
        if core == 1:
            orders[core, z, x, one, two] = (z + two) % RING * RING + (x + one) % RING
        else:
            orders[core, z, x, one, two] = (z + one) % RING * RING + (x + two) % RING
    return orders.reshape(2 * RING * RING, RING * RING)


def body(cache, span_latents, queries, selected, w_uv, w_out):
    seq_index = lax.axis_index("seq")
    mp_index = lax.axis_index("mp")
    y_index, core = seq_index // 2, seq_index % 2
    blocks_here, block_rows, latent_width = cache.shape
    token_count = queries.shape[0]
    groups_here = token_count // QG
    slots = groups_here * SEL

    order = lax.dynamic_index_in_dim(
        jnp.asarray(block_orders()), core * RING * RING + mp_index, 0, keepdims=False
    )
    selected, order = lax.optimization_barrier((selected, order))
    requests = selected.reshape(RING, 2, slots) - seq_index * blocks_here
    requests = jnp.roll(requests, -y_index, axis=0)
    requests = jnp.where(core == 0, requests, requests[:, ::-1])
    flat = jnp.concatenate(
        [
            cache[:, :, :KV_RANK].reshape(blocks_here, block_rows * KV_RANK),
            cache[:, :, KV_RANK:].reshape(blocks_here, block_rows * ROPE),
        ],
        axis=1,
    )

    picks = requests.transpose(1, 0, 2).reshape(-1)
    onehot = (picks[:, None] == lax.broadcasted_iota(jnp.int32, (1, blocks_here), 1)).astype(
        cache.dtype
    )
    rows = jnp.dot(onehot, flat, preferred_element_type=jnp.float32).astype(cache.dtype)
    rows = rows.reshape(2, RING, slots, block_rows * latent_width)
    both = rows[0] + along_core(rows[1])

    half = slots // 2
    own, up, far, down = both
    by_up = along_y(far[:half], 1)
    by_down = along_y(far[half:], 3)
    high_from_up = along_y(up[half:], 1)
    low_from_down = along_y(down[:half], 3)
    low_from_up = along_y(join(up[:half], by_up), 1)
    high_from_down = along_y(join(down[half:], by_down), 3)
    low = own[:half] + low_from_up + low_from_down
    high = own[half:] + high_from_up + high_from_down
    shard = jnp.concatenate([low, high], axis=0)

    others = [along_plane(shard, True, step) for step in (1, 3, 2)]
    ready = along_core(others[-1][:MARK, :MARK_LANES])
    lines = stack_lines([shard] + others, ready)

    local = span_latents.T
    planes = [[along_plane(part, False, step) for step in (1, 3)] for part in lines]
    states = [attend_first(queries, part, local, g) for g, part in enumerate(lines)]
    after = [state[1] for state in states]
    for plane in planes:
        low, high = halves(*plane, after)
        plane += [along_plane(low, False, 1), along_plane(high, False, 3)]
    outputs = [
        attend_rest(states[g], planes[g]) for g in range(groups_here)
    ]

    def add(*parts):
        total = functools.reduce(jnp.add, [part.astype(jnp.float32) for part in parts])
        return total.astype(jnp.bfloat16)

    ready = along_core(outputs[-1][:MARK, :MARK_LANES])
    near, far_low, far_high = project_far(order, outputs, w_uv, w_out, ready)
    by_up = along_plane(far_low, False, 1)
    by_down = along_plane(far_high, False, 3)
    own_low, own_high, up_low, up_high, down_low, down_high = project_near(
        near, w_out, [far_low, far_high]
    )
    high_from_up = along_plane(up_high, False, 1)
    low_from_down = along_plane(down_low, False, 3)
    low_from_up = along_plane(add(up_low, by_up), False, 1)
    high_from_down = along_plane(add(down_high, by_down), False, 3)
    low = add(own_low, low_from_up, low_from_down)
    high = add(own_high, high_from_up, high_from_down)

    own_rows = token_count // (RING * RING)
    parts = [low[:own_rows], low[own_rows:], high[:own_rows], high[own_rows:]]
    return add(parts[0], *[along_plane(parts[step], True, step) for step in (1, 3, 2)])


def solution(mesh):
    return jax.shard_map(
        body,
        mesh=mesh,
        in_specs=(
            P("seq", "mp", None),
            P("seq", None),
            P("seq", "mp"),
            P(),
            P("mp", None, None),
            P("mp", None),
        ),
        out_specs=P(("seq", "mp"), None),
        check_vma=False,
    )
```
